512 devices in a mesh: chan: 8 (over y_lo, core), seg: 64 (over y_hi, z, x).
Axes of the slice: x: 4, y: 8 (y_hi: 2, y_lo: 4; y = y_hi * 4 + y_lo), z: 8, core: 2. Of those that a mesh axis runs over, the one named last changes fastest.
Arguments:
- waveforms: bfloat16 [512, 512, 1536], P('seg', 'chan'), may hold values from -6 to 6
- segment_keep: int32 [512], P('seg'), may hold values 0 or 1
- channel_good: int32 [512], P('chan'), may hold values 0 or 1
Outputs:
- correlations: bfloat16 [512, 512, 2560], P('chan', 'seg')
The draws below stay inside these ranges and needn't reach their ends.
Inputs may be any that keep to these rules, and one draw needn't show every extreme that they name: `segment_keep`: 1 keeps the segment, 0 drops it. `channel_good`: 1 marks a working channel, 0 a dead one.
All inputs are finite; a program needn't handle non-finite values. No bound on the sum of `segment_keep` or of `channel_good` on one device may be relied on, other than what follows from the above.
Results may differ from the reference program's by a relative error of at most 0.0076.
Values may be sent and summed in bfloat16 or wider, within the bound.
A program may use at most 64 MiB of HBM per device.

```python
import math
import jax
import jax.numpy as jnp
from jax import lax

C = 512
NT = 1536
BAND_FREQ_BINS = 384
LOWEST_BAND_BIN = 12
LAGS = 2560
SEGS = 512
N_CHAN = 8


def set_ends(values, own_key, least, largest):
    shape = values.shape
    spot = [jax.random.randint(jax.random.fold_in(own_key, axis), (), 0, shape[axis]) for axis in range(len(shape))]
    values = values.at[tuple(spot)].set(least)
    longest = shape.index(max(shape))
    spot[longest] = (spot[longest] + 1) % shape[longest]
    return values.at[tuple(spot)].set(largest)


def block_scale(key, dims, shards, least, largest):
    gain, own = 1.0, jax.random.fold_in(key, 6)
    for position, shards_of in shards:
        heights = jnp.exp(jax.random.uniform(jax.random.fold_in(own, position), (shards_of,), jnp.float32, least / len(shards), largest / len(shards)))
        gain = gain * jnp.repeat(heights, dims[position] // shards_of).reshape([-1 if axis == position else 1 for axis in range(len(dims))])
    return gain


def bell_draw(rng, shape, scale, limit, cuts=(), kind=jnp.bfloat16):
    values = jax.random.normal(rng, shape, jnp.float32) * scale
    if len(cuts) > 0:
        values = block_scale(rng, shape, cuts, -0.22, 0.18) * values
    return jnp.clip(values, min=-limit, max=limit).astype(kind)


def setup_inputs(seed: int = 0) -> dict:
    seeds = jax.random.split(jax.random.key(seed), 4)
    return {
        "waveforms": bell_draw(seeds[0], (SEGS, C, NT), 1.0, 6.0, ((0, 64), (1, 8))),
        "segment_keep": set_ends((jax.random.randint(seeds[1], (SEGS,), 0, 8) < 7).astype(jnp.int32), jax.random.fold_in(seeds[1], 1), 0, 1),
        "channel_good": set_ends((jax.random.randint(seeds[2], (C,), 0, 16) < 15).astype(jnp.int32), jax.random.fold_in(seeds[2], 1), 0, 1),
    }


def forward_table():
    sample_ids = jnp.arange(NT, dtype=jnp.int32)
    bin_indices = LOWEST_BAND_BIN + jnp.arange(BAND_FREQ_BINS, dtype=jnp.int32)
    phase_ids = jnp.remainder(sample_ids[:, None] * bin_indices[None, :], 2 * NT)
    theta = 2.0 * math.pi / (2 * NT) * phase_ids.astype(jnp.float32)
    stacked = jnp.stack([jnp.cos(theta), -jnp.sin(theta)], axis=1) / math.sqrt(NT)
    return stacked.astype(jnp.bfloat16)

def lag_table():
    bin_indices = LOWEST_BAND_BIN + jnp.arange(BAND_FREQ_BINS, dtype=jnp.int32)
    lag_ids = jnp.arange(LAGS, dtype=jnp.int32) - LAGS // 2
    phase_ids = jnp.remainder(bin_indices[:, None] * lag_ids[None, :], 2 * NT)
    theta = 2.0 * math.pi / (2 * NT) * phase_ids.astype(jnp.float32)
    return jnp.stack([jnp.cos(theta), -jnp.sin(theta)], axis=1).astype(jnp.bfloat16)

def reference(waveforms, segment_keep, channel_good):
    block_width = C // N_CHAN
    spectra = jnp.dot(waveforms.reshape(SEGS * C, NT), forward_table().reshape(NT, 2 * BAND_FREQ_BINS), preferred_element_type=jnp.float32).reshape(SEGS, C, 2, BAND_FREQ_BINS)
    magnitude = jnp.sqrt(lax.optimization_barrier(jnp.sum(spectra * spectra, axis=2)))
    water_level = 0.5 * lax.optimization_barrier(jnp.mean(magnitude, axis=-1)) + 1e-06
    flags = segment_keep.astype(jnp.float32)[:, None] * channel_good.astype(jnp.float32)[None, :]
    weight = flags[:, :, None] / jnp.maximum(magnitude, water_level[:, :, None])
    whitened_spectra = (spectra * weight[:, :, None, :]).astype(jnp.bfloat16)
    every_real = whitened_spectra[:, :, 0, :].astype(jnp.float32)
    every_imag = whitened_spectra[:, :, 1, :].astype(jnp.float32)
    blocks = jnp.moveaxis(whitened_spectra.reshape(SEGS, N_CHAN, block_width, 2, BAND_FREQ_BINS), 1, 0)
    lag_values = lag_table().astype(jnp.float32)
    norm_divisor = 1.0 / math.sqrt(SEGS * BAND_FREQ_BINS)

    def one_block(item):
        block, block_position = item
        block_real = block[:, :, 0, :].astype(jnp.float32)
        block_imag = block[:, :, 1, :].astype(jnp.float32)
        real_part = jnp.einsum('saf,sbf->fab', block_real, every_real) + jnp.einsum('saf,sbf->fab', block_imag, every_imag)
        imag_part = jnp.einsum('saf,sbf->fab', block_imag, every_real) - jnp.einsum('saf,sbf->fab', block_real, every_imag)
        cross_sum = jnp.stack([real_part, imag_part], axis=1)
        own_ids = block_position * block_width + jnp.arange(block_width, dtype=jnp.int32)
        self_pair = own_ids[:, None] == jnp.arange(C, dtype=jnp.int32)[None, :]
        cross_spectra = jnp.where(self_pair[None, None], 0.0, cross_sum).astype(jnp.bfloat16)
        lagged = jnp.einsum('fpab,fpl->abl', cross_spectra.astype(jnp.float32), lag_values)
        return (lagged * norm_divisor).astype(jnp.bfloat16)
    result = lax.map(one_block, (blocks, jnp.arange(N_CHAN, dtype=jnp.int32)))
    return result.reshape(C, C, LAGS)
```

```python
import functools

import jax
import jax.numpy as jnp
import ml_dtypes
import numpy as np
from jax import lax
from jax.experimental import pallas as pl
from jax.experimental.pallas import tpu as pltpu
from jax.sharding import PartitionSpec as P

NT = 1536
BINS = 384
LOWEST = 12
LAGS = 2560
SEGS = 512
MESH = pl.DeviceIdType.MESH
F32 = jnp.float32
BF16 = jnp.bfloat16


def forward_rows():
    t = np.arange(NT, dtype=np.int64)
    f = LOWEST + np.arange(BINS, dtype=np.int64)
    theta = np.float32(2.0 * np.pi / (2 * NT)) * ((f[:, None] * t[None, :]) % (2 * NT)).astype(np.float32)
    theta = theta.astype(np.float64)
    rows = np.concatenate([np.cos(theta), -np.sin(theta)], axis=0) / np.sqrt(NT)
    return rows.astype(np.float32).astype(ml_dtypes.bfloat16)


def lag_rows():
    f = LOWEST + np.arange(BINS, dtype=np.int64)
    l = np.arange(LAGS, dtype=np.int64) - LAGS // 2
    phi = np.float32(2.0 * np.pi / (2 * NT)) * ((f[:, None] * l[None, :]) % (2 * NT)).astype(np.float32)
    phi = phi.astype(np.float64)
    rows = np.concatenate([np.cos(phi), -np.sin(phi)], axis=0)
    return rows.astype(np.float32).astype(ml_dtypes.bfloat16)


def device_of(row, column):
    y, core = row // 2, row % 2
    return ((y % 4) * 2 + core, (y // 4) * 32 + column)


def share(row, column):
    return (row // 2 + 2 * (row % 2) + column // 4 + column % 4) % 4


def column_slot(row, column):
    return (row % 2) * 6 + (row // 8) * 3 + share(row, column) - 1


def row_slot(row, column):
    return (column // 4) * 3 + share(row, column) - 1


def bin_place(f, core):
    in_0 = f < 192
    y0, slot24 = f // 24, f % 24
    z0, r0 = slot24 // 3, slot24 % 3
    x0 = (r0 + 1 - y0 - z0 + 32) % 4
    g = f - 192
    g = jnp.where(in_0, 0, g)
    c1, slot6 = g // 6, g % 6
    yh1, r1 = slot6 // 3, slot6 % 3
    yl1 = (r1 + 1 - 2 - c1 // 4 - c1 % 4 + 32) % 4
    place_0 = jnp.where(in_0, (z0 * 4 + x0) * 12 + (y0 // 4) * 3 + r0, c1 * 12 + 6 + slot6)
    place_1 = jnp.where(in_0, (y0 * 2) * 24 + slot24, ((yh1 * 4 + yl1) * 2 + 1) * 24 + (c1 // 4) * 3 + r1)
    return jnp.where(core == 0, place_0, place_1)


def stack_kernel(
    wave, table, keep, good, lhs_out,
    spec, mag, sent, mid_a, mid_b, got, gram_in, cross, back_a, back_b, done_a, done_b, rows_f, lhs_f,
    send_sem, recv_sem, local_sem,
):
    chan = lax.axis_index("chan")
    seg = lax.axis_index("seg")
    core = chan % 2
    y = (seg // 32) * 4 + chan // 2
    column = seg % 32
    z, x = column // 4, column % 4
    row = y * 2 + core
    y8 = (chan // 2) * 2 + seg // 32
    owner = share(row, column) != 0

    def next_column(k):
        return ((z + k // 4) % 8) * 4 + (x + k) % 4

    def next_row(k):
        return ((y + k // 2) % 8) * 2 + (core + k) % 2

    barrier = pltpu.get_barrier_semaphore()

    @pl.loop(1, 32)
    def _(k):
        pl.semaphore_signal(barrier, inc=1, device_id=device_of(row, next_column(k)), device_id_type=MESH)

    @pl.loop(1, 16)
    def _(k):
        pl.semaphore_signal(barrier, inc=1, device_id=device_of(next_row(k), column), device_id_type=MESH)

    def remote(src, dst, n, to_row, to_column):
        return pltpu.make_async_remote_copy(
            src_ref=src, dst_ref=dst, send_sem=send_sem.at[n], recv_sem=recv_sem.at[n],
            device_id=device_of(to_row, to_column), device_id_type=MESH,
        )

    def local(src, dst, n):
        return pltpu.make_async_copy(src, dst, local_sem.at[n])

    def wait_bytes(ref, sem):
        pltpu.make_async_copy(ref, ref, sem).wait()

    @pl.loop(0, 2)
    def _(half):
        cols = pl.ds(pl.multiple_of(half * 256, 256), 256)
        spec[:, cols] = lax.dot_general(
            table[...], wave[cols, :], (((1,), (1,)), ((), ())), preferred_element_type=F32
        )

    def add_magnitude(g, total):
        at = pl.multiple_of(g * 8, 8)
        re = spec[pl.ds(at, 8), :]
        im = spec[pl.ds(pl.multiple_of(BINS + at, 8), 8), :]
        m = jnp.sqrt(re * re + im * im)
        mag[pl.ds(at, 8), :] = m
        return total + m

    total = lax.fori_loop(0, BINS // 8, add_magnitude, jnp.zeros((8, 512), F32), unroll=4)
    water = 0.5 * (jnp.sum(total, axis=0, keepdims=True) * (1.0 / BINS)) + 1e-06
    good_f = good[...].astype(F32)
    good_2 = jnp.concatenate([good_f, good_f], axis=1)
    lane = lax.broadcasted_iota(jnp.int32, (1, 128), 1)
    lower = lane < 64
    flags = jnp.concatenate(
        [good_2 * jnp.where(lower, keep[2 * t].astype(F32), keep[2 * t + 1].astype(F32)) for t in range(4)], axis=1
    )
    lower8 = lax.broadcasted_iota(jnp.int32, (8, 128), 1) < 64

    @pl.loop(0, BINS // 8)
    def _(g):
        at = pl.multiple_of(g * 8, 8)
        weight = flags / jnp.maximum(mag[pl.ds(at, 8), :], water)
        re = spec[pl.ds(at, 8), :] * weight
        im = spec[pl.ds(pl.multiple_of(BINS + at, 8), 8), :] * weight
        by_s = []
        for t in range(4):
            r_t, i_t = re[:, 128 * t : 128 * t + 128], im[:, 128 * t : 128 * t + 128]
            by_s.append(jnp.where(lower8, r_t, pltpu.roll(i_t, 64, 1)))
            by_s.append(jnp.where(lower8, pltpu.roll(r_t, 64, 1), i_t))
        units = jnp.swapaxes(jnp.stack(by_s, axis=0), 0, 1)
        for k in range(8):
            sent[bin_place(g * 8 + k, core)] = units[k].astype(BF16)

    pl.semaphore_wait(barrier, 46)

    @pl.when(core == 0)
    def _():
        local(sent.at[pl.ds(column * 12, 12)], mid_a.at[column], 0).start()

        @pl.loop(1, 32)
        def _(k):
            to = next_column(k)
            remote(sent.at[pl.ds(to * 12, 12)], mid_a.at[column], 0, row, to).start()

    @pl.when(core == 1)
    def _():
        local(sent.at[pl.ds(row * 24, 24)], mid_b.at[y8], 1).start()

        @pl.loop(1, 16)
        def _(k):
            to = next_row(k)
            remote(sent.at[pl.ds(to * 24, 24)], mid_b.at[y8], 1, to, column).start()

    @pl.when(core == 0)
    def _():
        wait_bytes(mid_a.at[pl.ds(0, 31)], recv_sem.at[0])
        wait_bytes(mid_a.at[0], local_sem.at[0])

        @pl.loop(1, 16)
        def _(k):
            to = next_row(k)

            @pl.when(share(to, column) != 0)
            def _():
                remote(mid_a.at[:, column_slot(to, column)], got.at[0, y8], 2, to, column).start()

        @pl.when(owner)
        def _():
            local(mid_a.at[:, column_slot(row, column)], got.at[0, y8], 2).start()

        wait_bytes(mid_b, recv_sem.at[1])

    @pl.when(core == 1)
    def _():
        wait_bytes(mid_b.at[pl.ds(0, 7)], recv_sem.at[1])
        wait_bytes(mid_b.at[0], local_sem.at[1])

    @pl.loop(1, 32)
    def _(k):
        to = next_column(k)

        @pl.when(share(row, to) != 0)
        def _():
            remote(mid_b.at[:, row_slot(row, to)], got.at[1, :, column], 3, row, to).start()

    @pl.when(owner)
    def _():
        local(mid_b.at[:, row_slot(row, column)], got.at[1, :, column], 3).start()
        wait_bytes(got.at[1, :, 0], local_sem.at[3])
        wait_bytes(got.at[1, :, pl.ds(0, 31)], recv_sem.at[3])

        @pl.when(core == 0)
        def _():
            wait_bytes(got.at[0, 0], local_sem.at[2])
            wait_bytes(got.at[0, pl.ds(0, 7)], recv_sem.at[2])

        @pl.when(core == 1)
        def _():
            wait_bytes(got.at[0], recv_sem.at[2])

        for c in range(2):
            for yl in range(4):
                block = got[c, 2 * yl : 2 * yl + 2].astype(F32).reshape(512, 128).astype(BF16)
                gram_in[:, 128 * (4 * c + yl) : 128 * (4 * c + yl) + 128] = block
        sign = jnp.where(lower, 1.0, -1.0).astype(F32)
        b_ids = lax.broadcasted_iota(jnp.int32, (64, 128), 0)
        a_ids = lax.broadcasted_iota(jnp.int32, (64, 128), 1) % 64

        @pl.loop(0, 4)
        def _(pair):
            products = lax.dot_general(
                gram_in[:, pl.ds(pl.multiple_of(pair * 256, 256), 256)], gram_in[...],
                (((0,), (0,)), ((), ())), preferred_element_type=F32,
            )
            for second in range(2):
                i = pair * 2 + second
                chan_b = (i % 4) * 2 + i // 4
                for j in range(8):
                    chan_a = (j % 4) * 2 + j // 4
                    tile = products[128 * second : 128 * second + 128, 128 * j : 128 * j + 128]
                    summed = tile[:64] + sign * pltpu.roll(tile[64:], 64, 1)
                    summed = jnp.where(jnp.logical_and(b_ids == a_ids, i == j), 0.0, summed)
                    for part in range(8):
                        seg_b = chan_b * 8 + part
                        to_row = ((seg_b // 32) * 4 + chan_a // 2) * 2 + chan_a % 2
                        to_column = seg_b % 32
                        place = jnp.where(core == 0, to_column * 16 + to_row, to_row * 32 + to_column)
                        cross[place] = summed[8 * part : 8 * part + 8].astype(BF16)

        @pl.when(core == 0)
        def _():
            slot = row_slot(row, column)
            local(cross.at[pl.ds(column * 16, 16)], back_a.at[slot], 4).start()

            @pl.loop(1, 32)
            def _(k):
                to = next_column(k)
                remote(cross.at[pl.ds(to * 16, 16)], back_a.at[slot], 4, row, to).start()

        @pl.when(core == 1)
        def _():
            slot = column_slot(row, column) - 6
            local(cross.at[pl.ds(row * 32, 32)], back_b.at[slot], 5).start()

            @pl.loop(1, 16)
            def _(k):
                to = next_row(k)
                remote(cross.at[pl.ds(to * 32, 32)], back_b.at[slot], 5, to, column).start()

    @pl.when(core == 0)
    def _():
        @pl.when(owner)
        def _():
            wait_bytes(back_a.at[0], local_sem.at[4])
            wait_bytes(back_a.at[pl.ds(0, 23)], recv_sem.at[4])

        @pl.when(jnp.logical_not(owner))
        def _():
            wait_bytes(back_a, recv_sem.at[4])

        @pl.loop(1, 16)
        def _(k):
            to = next_row(k)
            remote(back_a.at[:, to], done_a.at[y], 6, to, column).start()

        local(back_a.at[:, row], done_a.at[y], 6).start()

    own_back = jnp.logical_and(owner, core == 1)

    @pl.when(own_back)
    def _():
        wait_bytes(back_b.at[0], local_sem.at[5])
        wait_bytes(back_b.at[pl.ds(0, 5)], recv_sem.at[5])

    @pl.when(jnp.logical_not(own_back))
    def _():
        wait_bytes(back_b, recv_sem.at[5])

    @pl.loop(1, 32)
    def _(k):
        to = next_column(k)
        remote(back_b.at[:, to], done_b.at[column], 7, row, to).start()

    local(back_b.at[:, column], done_b.at[column], 7).start()

    @pl.when(core == 0)
    def _():
        wait_bytes(done_a.at[0], local_sem.at[6])
        wait_bytes(done_a.at[pl.ds(0, 7)], recv_sem.at[6])

    @pl.when(core == 1)
    def _():
        wait_bytes(done_a, recv_sem.at[6])

    wait_bytes(done_b.at[0], local_sem.at[7])
    wait_bytes(done_b.at[pl.ds(0, 31)], recv_sem.at[7])

    rows_f[0:1536] = done_a[...].astype(F32).reshape(1536, 128)
    rows_f[1536:3072] = done_b[...].astype(F32).reshape(1536, 128)
    for b in range(8):
        turned = rows_f[pl.ds(b, BINS, stride=8), :].T
        for p in range(2):
            for k in range(3):
                lhs_f[3 * p + k, pl.ds(b, 64, stride=8), :] = turned[64 * p : 64 * p + 64, 128 * k : 128 * k + 128]
    for k in range(6):
        lhs_out[:, 128 * k : 128 * k + 128] = lhs_f[k].astype(BF16)

    @pl.when(core == 0)
    def _():
        wait_bytes(mid_a.at[pl.ds(0, 31)], send_sem.at[0])

        @pl.when(owner)
        def _():
            wait_bytes(got.at[0, pl.ds(0, 8)], send_sem.at[2])
            wait_bytes(got.at[0, pl.ds(0, 3)], send_sem.at[2])
            wait_bytes(cross.at[pl.ds(0, 31 * 16)], send_sem.at[4])

        @pl.when(jnp.logical_not(owner))
        def _():
            wait_bytes(got.at[0, pl.ds(0, 8)], send_sem.at[2])
            wait_bytes(got.at[0, pl.ds(0, 4)], send_sem.at[2])

        wait_bytes(done_a.at[pl.ds(0, 8)], send_sem.at[6])
        wait_bytes(done_a.at[pl.ds(0, 7)], send_sem.at[6])

    @pl.when(core == 1)
    def _():
        wait_bytes(sent.at[pl.ds(0, 15 * 24)], send_sem.at[1])

        @pl.when(owner)
        def _():
            wait_bytes(cross.at[pl.ds(0, 15 * 32)], send_sem.at[5])

    @pl.when(owner)
    def _():
        wait_bytes(got.at[1, :, pl.ds(0, 23)], send_sem.at[3])

    @pl.when(jnp.logical_not(owner))
    def _():
        wait_bytes(got.at[1, :, pl.ds(0, 24)], send_sem.at[3])

    wait_bytes(done_b.at[pl.ds(0, 31)], send_sem.at[7])


def stacked(wave, table, keep, good):
    vmem = pl.BlockSpec(memory_space=pltpu.VMEM)
    return pl.pallas_call(
        stack_kernel,
        out_shape=jax.ShapeDtypeStruct((512, 2 * BINS), BF16),
        in_specs=[vmem, vmem, pl.BlockSpec(memory_space=pltpu.SMEM), vmem],
        out_specs=vmem,
        scratch_shapes=[
            pltpu.VMEM((2 * BINS, 512), F32),
            pltpu.VMEM((BINS, 512), F32),
            pltpu.VMEM((BINS, 8, 128), BF16),
            pltpu.VMEM((32, 12, 8, 128), BF16),
            pltpu.VMEM((8, 24, 8, 128), BF16),
            pltpu.VMEM((2, 8, 32, 8, 128), BF16),
            pltpu.VMEM((512, 1024), BF16),
            pltpu.VMEM((512, 8, 128), BF16),
            pltpu.VMEM((24, 16, 8, 128), BF16),
            pltpu.VMEM((6, 32, 8, 128), BF16),
            pltpu.VMEM((8, 24, 8, 128), BF16),
            pltpu.VMEM((32, 6, 8, 128), BF16),
            pltpu.VMEM((3072, 128), F32),
            pltpu.VMEM((6, 512, 128), F32),
            pltpu.SemaphoreType.DMA((8,)),
            pltpu.SemaphoreType.DMA((8,)),
            pltpu.SemaphoreType.DMA((8,)),
        ],
        compiler_params=pltpu.CompilerParams(collective_id=0, has_side_effects=True, vmem_limit_bytes=48 << 20),
        name="stack_cross_spectra",
    )(wave, table, keep, good)


def lag_kernel(scale, lhs, table, out):
    values = jnp.dot(lhs[...], table[...], preferred_element_type=F32) * scale
    out[...] = values.reshape(64, 8, values.shape[1]).astype(BF16)


def lagged(lhs, table, scale):
    width = 512
    return pl.pallas_call(
        functools.partial(lag_kernel, scale),
        grid=(LAGS // width,),
        out_shape=jax.ShapeDtypeStruct((64, 8, LAGS), BF16),
        in_specs=[
            pl.BlockSpec((512, 2 * BINS), lambda i: (0, 0)),
            pl.BlockSpec((2 * BINS, width), lambda i: (0, i)),
        ],
        out_specs=pl.BlockSpec((64, 8, width), lambda i: (0, 0, i)),
        compiler_params=pltpu.CompilerParams(vmem_limit_bytes=48 << 20),
        name="lag_transform",
    )(lhs, table)


def local(waveforms, segment_keep, channel_good):
    wave = waveforms.reshape(512, NT)
    lhs = stacked(wave, jnp.asarray(forward_rows()), segment_keep, channel_good.reshape(1, 64))
    return lagged(lhs, jnp.asarray(lag_rows()), float(1.0 / np.sqrt(SEGS * BINS)))


def solution(mesh):
    placed = (P("seg", "chan", None), P("seg"), P("chan"))
    return jax.shard_map(
        local, mesh=mesh, in_specs=placed, out_specs=P("chan", "seg", None), check_vma=False
    )
```

```python
import functools

import jax
import jax.numpy as jnp
import ml_dtypes
import numpy as np
from jax import lax
from jax.experimental import pallas as pl
from jax.experimental.pallas import tpu as pltpu
from jax.sharding import PartitionSpec as P

NT = 1536
BINS = 384
LOWEST = 12
LAGS = 2560
SEGS = 512
MESH = pl.DeviceIdType.MESH
F32 = jnp.float32
BF16 = jnp.bfloat16


def forward_rows():
    t = np.arange(NT, dtype=np.int64)
    f = LOWEST + np.arange(BINS, dtype=np.int64)
    theta = np.float32(2.0 * np.pi / (2 * NT)) * ((f[:, None] * t[None, :]) % (2 * NT)).astype(np.float32)
    theta = theta.astype(np.float64)
    rows = np.concatenate([np.cos(theta), -np.sin(theta)], axis=0) / np.sqrt(NT)
    return rows.astype(np.float32).astype(ml_dtypes.bfloat16)


def lag_rows():
    f = LOWEST + np.arange(BINS, dtype=np.int64)
    l = np.arange(LAGS, dtype=np.int64) - LAGS // 2
    phi = np.float32(2.0 * np.pi / (2 * NT)) * ((f[:, None] * l[None, :]) % (2 * NT)).astype(np.float32)
    phi = phi.astype(np.float64)
    rows = np.concatenate([np.cos(phi), -np.sin(phi)], axis=0)
    return rows.astype(np.float32).astype(ml_dtypes.bfloat16)


def device_of(row, column):
    y, core = row // 2, row % 2
    return ((y % 4) * 2 + core, (y // 4) * 32 + column)


def share(row, column):
    return (row // 2 + 2 * (row % 2) + column // 4 + column % 4) % 4


def column_slot(row, column):
    return (row % 2) * 6 + (row // 8) * 3 + share(row, column) - 1


def row_slot(row, column):
    return (column // 4) * 3 + share(row, column) - 1


def row_slot_by_parity(row, column):
    z = column // 4
    return (z % 2) * 12 + (z // 2) * 3 + share(row, column) - 1


def ring_8(k):
    return jnp.where(k % 2 == 1, (k + 1) // 2, (8 - k // 2) % 8)


def ring_4(k):
    return jnp.where(k == 2, 3, jnp.where(k == 3, 2, k))


def make_units(core, wave, table, keep, good, spec, mag, turn, sent):
    @pl.loop(0, 2)
    def _(half):
        cols = pl.ds(pl.multiple_of(half * 256, 256), 256)
        spec[:, cols] = lax.dot_general(
            table[...], wave[cols, :], (((1,), (1,)), ((), ())), preferred_element_type=F32
        )

    def add_magnitude(g, total):
        at = pl.multiple_of(g * 8, 8)
        re = spec[pl.ds(at, 8), :]
        im = spec[pl.ds(pl.multiple_of(BINS + at, 8), 8), :]
        m = jnp.sqrt(re * re + im * im)
        mag[pl.ds(at, 8), :] = m
        return total + m

    total = lax.fori_loop(0, BINS // 8, add_magnitude, jnp.zeros((8, 512), F32), unroll=4)
    water = 0.5 * (jnp.sum(total, axis=0, keepdims=True) * (1.0 / BINS)) + 1e-06
    good_f = good[...].astype(F32)
    good_2 = jnp.concatenate([good_f, good_f], axis=1)
    lower = lax.broadcasted_iota(jnp.int32, (1, 128), 1) < 64
    flags = jnp.concatenate(
        [good_2 * jnp.where(lower, keep[2 * t].astype(F32), keep[2 * t + 1].astype(F32)) for t in range(4)], axis=1
    )
    lower8 = lax.broadcasted_iota(jnp.int32, (8, 128), 1) < 64

    def whiten_8(at):
        weight = flags / jnp.maximum(mag[pl.ds(at, 8), :], water)
        re = spec[pl.ds(at, 8), :] * weight
        im = spec[pl.ds(pl.multiple_of(BINS + at, 8), 8), :] * weight
        rows = pl.multiple_of(at * 8, 64)
        for t in range(4):
            r_t, i_t = re[:, 128 * t : 128 * t + 128], im[:, 128 * t : 128 * t + 128]
            turn[pl.ds(rows + 2 * t, 8, stride=8), :] = jnp.where(lower8, r_t, pltpu.roll(i_t, 64, 1))
            turn[pl.ds(rows + 2 * t + 1, 8, stride=8), :] = jnp.where(lower8, pltpu.roll(r_t, 64, 1), i_t)

    def put(at, k, place):
        sent[place] = turn[pl.ds(pl.multiple_of(at * 8 + 8 * k, 8), 8), :].astype(BF16)

    on_0 = core == 0

    @pl.loop(0, 8)
    def _(y0):
        for block in range(3):
            at = pl.multiple_of(y0 * 24 + 8 * block, 8)
            whiten_8(at)
            for k in range(8):
                slot = 8 * block + k
                z0, r0 = slot // 3, slot % 3
                x0 = (r0 + 1 - z0 + 32 - y0) % 4
                place_0 = x0 * 12 + (y0 // 4) * 3 + (z0 * 48 + r0)
                place_1 = y0 * 48 + ((z0 % 2) * 12 + (z0 // 2) * 3 + r0)
                put(at, k, jnp.where(on_0, place_0, place_1))

    @pl.loop(0, 8)
    def _(z1):
        for block in range(3):
            at = pl.multiple_of(192 + z1 * 24 + 8 * block, 8)
            whiten_8(at)
            for k in range(8):
                x1, slot = (8 * block + k) // 6, (8 * block + k) % 6
                yh1, r1 = slot // 3, slot % 3
                yl1 = (r1 + 1 - 2 - x1 + 32 - z1) % 4
                place_0 = z1 * 48 + (x1 * 12 + 6 + slot)
                place_1 = yl1 * 48 + (z1 % 2) * 12 + (z1 // 2) * 3 + (yh1 * 192 + 24 + r1)
                put(at, k, jnp.where(on_0, place_0, place_1))


def gather_blocks(got, gram_in):
    for c in range(2):
        for yl in range(4):
            block = got[c, 2 * yl : 2 * yl + 2].astype(F32).reshape(512, 128).astype(BF16)
            gram_in[:, 128 * (4 * c + yl) : 128 * (4 * c + yl) + 128] = block


def block_of(chan):
    return (chan % 2) * 4 + chan // 2


def cross_of(core, chans, gram_in, cross):
    sign = jnp.where(lax.broadcasted_iota(jnp.int32, (1, 128), 1) < 64, 1.0, -1.0).astype(F32)
    b_ids = lax.broadcasted_iota(jnp.int32, (64, 128), 0)
    a_ids = lax.broadcasted_iota(jnp.int32, (64, 128), 1) % 64
    same = b_ids == a_ids
    ids = [block_of(chan) for chan in chans]
    left = jnp.concatenate(
        [gram_in[:, pl.ds(pl.multiple_of(i * 128, 128), 128)] for i in ids], axis=1
    )
    products = lax.dot_general(left, gram_in[...], (((0,), (0,)), ((), ())), preferred_element_type=F32)
    for second in range(2):
        seg_b = chans[second] * 8
        to_y, to_column = (seg_b // 32) * 4, seg_b % 32
        base = jnp.where(core == 0, to_column * 16 + to_y * 2, to_y * 64 + to_column)
        step_part = jnp.where(core == 0, 16, 1)
        step_row = jnp.where(core == 0, 1, 32)
        for j in range(8):
            tile = products[128 * second : 128 * second + 128, 128 * j : 128 * j + 128]
            summed = tile[:64] + sign * pltpu.roll(tile[64:], 64, 1)
            summed = jnp.where(jnp.logical_and(same, ids[second] == j), 0.0, summed)
            chan_a = (j % 4) * 2 + j // 4
            at = base + step_row * chan_a
            for part in range(8):
                cross[at + step_part * part] = summed[8 * part : 8 * part + 8].astype(BF16)


def make_lhs(done_a, done_b, rows_f, lhs_f, lhs_out):
    rows_f[0:1536] = done_a[...].astype(F32).reshape(1536, 128)
    rows_f[1536:3072] = done_b[...].astype(F32).reshape(1536, 128)
    for b in range(8):
        turned = rows_f[pl.ds(b, BINS, stride=8), :].T
        for p in range(2):
            for k in range(3):
                lhs_f[3 * p + k, pl.ds(b, 64, stride=8), :] = turned[64 * p : 64 * p + 64, 128 * k : 128 * k + 128]
    for k in range(6):
        lhs_out[:, 128 * k : 128 * k + 128] = lhs_f[k].astype(BF16)


def stack_kernel(
    wave_hbm, table_hbm, keep_hbm, good_hbm, lhs_out,
    wave, table, keep, good,
    spec, mag, turn, sent, mid_a, mid_b, got, gram_in, cross, back_a, back_b, done_a, done_b, rows_f, lhs_f,
    send_sem, recv_sem, local_sem, load_sem,
):
    chan = lax.axis_index("chan")
    seg = lax.axis_index("seg")
    core = chan % 2
    y = (seg // 32) * 4 + chan // 2
    column = seg % 32
    z, x = column // 4, column % 4
    row = y * 2 + core
    y8 = (chan // 2) * 2 + seg // 32
    owner = share(row, column) != 0

    loads = [
        pltpu.make_async_copy(src, dst, load_sem.at[n])
        for n, (src, dst) in enumerate(((table_hbm, table), (wave_hbm, wave), (keep_hbm, keep), (good_hbm, good)))
    ]
    for load in loads:
        load.start()

    def next_column(k):
        k = 32 - k
        return ((z + ring_8(k % 8)) % 8) * 4 + (x + ring_4(k // 8)) % 4

    def next_row(k):
        k = 16 - k
        return ((y + ring_8(k % 8)) % 8) * 2 + (core + k // 8) % 2

    barrier = pltpu.get_barrier_semaphore()

    @pl.loop(1, 32)
    def _(k):
        pl.semaphore_signal(barrier, inc=1, device_id=device_of(row, next_column(k)), device_id_type=MESH)

    @pl.loop(1, 16)
    def _(k):
        pl.semaphore_signal(barrier, inc=1, device_id=device_of(next_row(k), column), device_id_type=MESH)

    def remote(src, dst, n, m, to_row, to_column):
        return pltpu.make_async_remote_copy(
            src_ref=src, dst_ref=dst, send_sem=send_sem.at[n], recv_sem=recv_sem.at[m],
            device_id=device_of(to_row, to_column), device_id_type=MESH,
        )

    def local(src, dst, n):
        return pltpu.make_async_copy(src, dst, local_sem.at[n])

    def wait_bytes(ref, sem):
        pltpu.make_async_copy(ref, ref, sem).wait()

    for load in loads:
        load.wait()
    make_units(core, wave, table, keep, good, spec, mag, turn, sent)

    pl.semaphore_wait(barrier, 46)

    @pl.when(core == 0)
    def _():
        local(sent.at[pl.ds(column * 12, 12)], mid_a.at[column], 0).start()
        for c in range(2):
            @pl.loop(1, 32)
            def _(k):
                to = next_column(k)
                remote(sent.at[pl.ds(to * 12 + 6 * c, 6)], mid_a.at[column, pl.ds(6 * c, 6)], 0, c, row, to).start()

    @pl.when(core == 1)
    def _():
        local(sent.at[pl.ds(row * 24, 24)], mid_b.at[y8], 1).start()
        for c in range(2):
            @pl.loop(1, 16)
            def _(k):
                to = next_row(k)
                remote(sent.at[pl.ds(to * 24 + 12 * c, 12)], mid_b.at[y8, pl.ds(12 * c, 12)], 1, 2 + c, to, column).start()

    @pl.when(core == 0)
    def _():
        wait_bytes(mid_a.at[0], local_sem.at[0])

    @pl.when(core == 1)
    def _():
        wait_bytes(mid_b.at[0], local_sem.at[1])

    for c in range(2):
        @pl.when(core == 0)
        def _():
            wait_bytes(mid_a.at[pl.ds(0, 31), pl.ds(0, 6)], recv_sem.at[c])

            @pl.loop(0, 8)
            def _(k):
                to = ((y + ring_8(7 - k)) % 8) * 2 + c

                @pl.when(jnp.logical_and(share(to, column) != 0, to != row))
                def _():
                    remote(mid_a.at[:, column_slot(to, column)], got.at[0, y8], 2, 4, to, column).start()

            wait_bytes(mid_b.at[:, pl.ds(0, 12)], recv_sem.at[2 + c])

        @pl.when(core == 1)
        def _():
            wait_bytes(mid_b.at[pl.ds(0, 7), pl.ds(0, 12)], recv_sem.at[2 + c])

        @pl.loop(0, 16)
        def _(k):
            back = 15 - k
            to = ((z + (z + c) % 2 + 2 * ring_4(back % 4)) % 8) * 4 + (x + ring_4(back // 4)) % 4

            @pl.when(jnp.logical_and(share(row, to) != 0, to != column))
            def _():
                remote(mid_b.at[:, row_slot_by_parity(row, to)], got.at[1, :, column], 3, 5, row, to).start()

    @pl.when(owner)
    def _():
        @pl.when(core == 0)
        def _():
            local(mid_a.at[:, column_slot(row, column)], got.at[0, y8], 2).start()

        local(mid_b.at[:, row_slot_by_parity(row, column)], got.at[1, :, column], 3).start()
        wait_bytes(got.at[1, :, 0], local_sem.at[3])
        wait_bytes(got.at[1, :, pl.ds(0, 31)], recv_sem.at[5])

        @pl.when(core == 0)
        def _():
            wait_bytes(got.at[0, 0], local_sem.at[2])
            wait_bytes(got.at[0, pl.ds(0, 7)], recv_sem.at[4])

        @pl.when(core == 1)
        def _():
            wait_bytes(got.at[0], recv_sem.at[4])

        gather_blocks(got, gram_in)
        slot_a = row_slot(row, column)
        slot_b = column_slot(row, column) % 6

        @pl.loop(0, 4)
        def _(quarter):
            pair = (quarter + z // 2) % 4
            part = (quarter + 2 * (1 - y // 4)) % 4
            first = jnp.where(core == 0, pair, 2 * part)
            second = jnp.where(core == 0, pair + 4, 2 * part + 1)
            cross_of(core, (first, second), gram_in, cross)

            @pl.when(core == 0)
            def _():
                @pl.loop(0, 8)
                def _(k):
                    to = pair * 8 + (column + k + 1) % 8

                    @pl.when(to != column)
                    def _():
                        remote(cross.at[pl.ds(to * 16, 16)], back_a.at[slot_a], 4, 6, row, to).start()

                    @pl.when(to == column)
                    def _():
                        local(cross.at[pl.ds(to * 16, 16)], back_a.at[slot_a], 4).start()

            @pl.when(core == 1)
            def _():
                half = (part % 2) * 16

                @pl.loop(0, 8)
                def _(k):
                    to = (part // 2) * 8 + (row + k + 1) % 8

                    @pl.when(to != row)
                    def _():
                        remote(
                            cross.at[pl.ds(to * 32 + half, 16)], back_b.at[slot_b, pl.ds(half, 16)], 5, 7, to, column
                        ).start()

                    @pl.when(to == row)
                    def _():
                        local(cross.at[pl.ds(to * 32 + half, 16)], back_b.at[slot_b, pl.ds(half, 16)], 5).start()

    @pl.when(core == 0)
    def _():
        @pl.when(owner)
        def _():
            wait_bytes(back_a.at[0], local_sem.at[4])
            wait_bytes(back_a.at[pl.ds(0, 23)], recv_sem.at[6])

        @pl.when(jnp.logical_not(owner))
        def _():
            wait_bytes(back_a, recv_sem.at[6])

        @pl.loop(1, 16)
        def _(k):
            to = next_row(k)
            remote(back_a.at[:, to], done_a.at[y], 6, 8, to, column).start()

        local(back_a.at[:, row], done_a.at[y], 6).start()

    own_back = jnp.logical_and(owner, core == 1)

    @pl.when(own_back)
    def _():
        wait_bytes(back_b.at[0], local_sem.at[5])
        wait_bytes(back_b.at[pl.ds(0, 5)], recv_sem.at[7])

    @pl.when(jnp.logical_not(own_back))
    def _():
        wait_bytes(back_b, recv_sem.at[7])

    @pl.loop(1, 32)
    def _(k):
        to = next_column(k)
        remote(back_b.at[:, to], done_b.at[column], 7, 9, row, to).start()

    local(back_b.at[:, column], done_b.at[column], 7).start()

    @pl.when(core == 0)
    def _():
        wait_bytes(done_a.at[0], local_sem.at[6])
        wait_bytes(done_a.at[pl.ds(0, 7)], recv_sem.at[8])

    @pl.when(core == 1)
    def _():
        wait_bytes(done_a, recv_sem.at[8])

    wait_bytes(done_b.at[0], local_sem.at[7])
    wait_bytes(done_b.at[pl.ds(0, 31)], recv_sem.at[9])
    make_lhs(done_a, done_b, rows_f, lhs_f, lhs_out)

    @pl.when(core == 0)
    def _():
        wait_bytes(mid_a.at[pl.ds(0, 31)], send_sem.at[0])

        @pl.when(owner)
        def _():
            wait_bytes(got.at[0, pl.ds(0, 8)], send_sem.at[2])
            wait_bytes(got.at[0, pl.ds(0, 3)], send_sem.at[2])
            wait_bytes(cross.at[pl.ds(0, 31 * 16)], send_sem.at[4])

        @pl.when(jnp.logical_not(owner))
        def _():
            wait_bytes(got.at[0, pl.ds(0, 8)], send_sem.at[2])
            wait_bytes(got.at[0, pl.ds(0, 4)], send_sem.at[2])

        wait_bytes(done_a.at[pl.ds(0, 8)], send_sem.at[6])
        wait_bytes(done_a.at[pl.ds(0, 7)], send_sem.at[6])

    @pl.when(core == 1)
    def _():
        wait_bytes(sent.at[pl.ds(0, 15 * 24)], send_sem.at[1])

        @pl.when(owner)
        def _():
            wait_bytes(cross.at[pl.ds(0, 15 * 32)], send_sem.at[5])

    @pl.when(owner)
    def _():
        wait_bytes(got.at[1, :, pl.ds(0, 23)], send_sem.at[3])

    @pl.when(jnp.logical_not(owner))
    def _():
        wait_bytes(got.at[1, :, pl.ds(0, 24)], send_sem.at[3])

    wait_bytes(done_b.at[pl.ds(0, 31)], send_sem.at[7])


def stacked(wave, table, keep, good):
    anywhere = pl.BlockSpec(memory_space=pl.ANY)
    return pl.pallas_call(
        stack_kernel,
        out_shape=jax.ShapeDtypeStruct((512, 2 * BINS), BF16),
        in_specs=[anywhere] * 4,
        out_specs=pl.BlockSpec(memory_space=pltpu.VMEM),
        scratch_shapes=[
            pltpu.VMEM((512, NT), BF16),
            pltpu.VMEM((2 * BINS, NT), BF16),
            pltpu.SMEM((8,), jnp.int32),
            pltpu.VMEM((1, 64), jnp.int32),
            pltpu.VMEM((2 * BINS, 512), F32),
            pltpu.VMEM((BINS, 512), F32),
            pltpu.VMEM((BINS * 8, 128), F32),
            pltpu.VMEM((BINS, 8, 128), BF16),
            pltpu.VMEM((32, 12, 8, 128), BF16),
            pltpu.VMEM((8, 24, 8, 128), BF16),
            pltpu.VMEM((2, 8, 32, 8, 128), BF16),
            pltpu.VMEM((512, 1024), BF16),
            pltpu.VMEM((512, 8, 128), BF16),
            pltpu.VMEM((24, 16, 8, 128), BF16),
            pltpu.VMEM((6, 32, 8, 128), BF16),
            pltpu.VMEM((8, 24, 8, 128), BF16),
            pltpu.VMEM((32, 6, 8, 128), BF16),
            pltpu.VMEM((3072, 128), F32),
            pltpu.VMEM((6, 512, 128), F32),
            pltpu.SemaphoreType.DMA((8,)),
            pltpu.SemaphoreType.DMA((10,)),
            pltpu.SemaphoreType.DMA((8,)),
            pltpu.SemaphoreType.DMA((4,)),
        ],
        compiler_params=pltpu.CompilerParams(collective_id=0, has_side_effects=True, vmem_limit_bytes=48 << 20),
        name="stack_cross_spectra",
    )(wave, table, keep, good)


def lag_kernel(scale, lhs, table, out, block, sem):
    width = block.shape[-1]
    count = LAGS // width
    for n in range(count):
        if n >= 2:
            pltpu.make_async_copy(block.at[n % 2], out.at[:, :, pl.ds((n - 2) * width, width)], sem.at[n % 2]).wait()
        values = jnp.dot(lhs[...], table[:, n * width : (n + 1) * width], preferred_element_type=F32) * scale
        block[n % 2] = values.reshape(64, 8, width).astype(BF16)
        pltpu.make_async_copy(block.at[n % 2], out.at[:, :, pl.ds(n * width, width)], sem.at[n % 2]).start()
    for n in range(count - 2, count):
        pltpu.make_async_copy(block.at[n % 2], out.at[:, :, pl.ds(n * width, width)], sem.at[n % 2]).wait()


def lagged(lhs, table, scale):
    vmem = pl.BlockSpec(memory_space=pltpu.VMEM)
    return pl.pallas_call(
        functools.partial(lag_kernel, scale),
        out_shape=jax.ShapeDtypeStruct((64, 8, LAGS), BF16),
        in_specs=[vmem, vmem],
        out_specs=pl.BlockSpec(memory_space=pl.ANY),
        scratch_shapes=[pltpu.VMEM((2, 64, 8, 512), BF16), pltpu.SemaphoreType.DMA((2,))],
        compiler_params=pltpu.CompilerParams(vmem_limit_bytes=48 << 20),
        name="lag_transform",
    )(lhs, table)


def local(waveforms, segment_keep, channel_good):
    wave = waveforms.reshape(512, NT)
    lhs = stacked(wave, jnp.asarray(forward_rows()), segment_keep, channel_good.reshape(1, 64))
    return lagged(lhs, jnp.asarray(lag_rows()), float(1.0 / np.sqrt(SEGS * BINS)))


def solution(mesh):
    placed = (P("seg", "chan", None), P("seg"), P("chan"))
    return jax.shard_map(
        local, mesh=mesh, in_specs=placed, out_specs=P("chan", "seg", None), check_vma=False
    )
```

```python
import functools

import jax
import jax.numpy as jnp
import ml_dtypes
import numpy as np
from jax import lax
from jax.experimental import pallas as pl
from jax.experimental.pallas import tpu as pltpu
from jax.sharding import PartitionSpec as P

NT = 1536
BINS = 384
LOWEST = 12
LAGS = 2560
SEGS = 512
MESH = pl.DeviceIdType.MESH
F32 = jnp.float32
BF16 = jnp.bfloat16


def forward_rows():
    t = np.arange(NT, dtype=np.int64)
    f = LOWEST + np.arange(BINS, dtype=np.int64)
    theta = np.float32(2.0 * np.pi / (2 * NT)) * ((f[:, None] * t[None, :]) % (2 * NT)).astype(np.float32)
    theta = theta.astype(np.float64)
    rows = np.concatenate([np.cos(theta), -np.sin(theta)], axis=0) / np.sqrt(NT)
    return rows.astype(np.float32).astype(ml_dtypes.bfloat16)


def lag_rows():
    f = LOWEST + np.arange(BINS, dtype=np.int64)
    l = np.arange(LAGS, dtype=np.int64) - LAGS // 2
    phi = np.float32(2.0 * np.pi / (2 * NT)) * ((f[:, None] * l[None, :]) % (2 * NT)).astype(np.float32)
    phi = phi.astype(np.float64)
    rows = np.concatenate([np.cos(phi), -np.sin(phi)], axis=0)
    return rows.astype(np.float32).astype(ml_dtypes.bfloat16)


def device_of(row, column):
    y, core = row // 2, row % 2
    return ((y % 4) * 2 + core, (y // 4) * 32 + column)


def share(row, column):
    return (row // 2 + 2 * (row % 2) + column // 4 + column % 4) % 4


def column_slot(row, column):
    return (row % 2) * 6 + (row // 8) * 3 + share(row, column) - 1


def row_slot(row, column):
    return (column // 4) * 3 + share(row, column) - 1


def row_slot_by_parity(row, column):
    z = column // 4
    return (z % 2) * 12 + (z // 2) * 3 + share(row, column) - 1


def turned_column(column):
    return ((column // 8) % 2) * 16 + (column // 16) * 8 + column % 8


def ring_8(k):
    return jnp.where(k % 2 == 1, (k + 1) // 2, (8 - k // 2) % 8)


def ring_4(k):
    return jnp.where(k == 2, 3, jnp.where(k == 3, 2, k))


def make_units(core, wave, table, keep, good, spec, mag, turn, sent, loaded=None, between=None):
    for third in range(3):
        if loaded is not None:
            loaded(third)
        rows = slice(256 * third, 256 * third + 256)
        spec[rows, :] = lax.dot_general(
            table[rows, :], wave[...], (((1,), (1,)), ((), ())), preferred_element_type=F32
        )

    def add_magnitude(g, total):
        at = pl.multiple_of(g * 8, 8)
        re = spec[pl.ds(at, 8), :]
        im = spec[pl.ds(pl.multiple_of(BINS + at, 8), 8), :]
        m = jnp.sqrt(re * re + im * im)
        mag[pl.ds(at, 8), :] = m
        return total + m

    total = lax.fori_loop(0, BINS // 8, add_magnitude, jnp.zeros((8, 512), F32), unroll=4)
    water = 0.5 * (jnp.sum(total, axis=0, keepdims=True) * (1.0 / BINS)) + 1e-06
    good_f = good[...].astype(F32)
    good_2 = jnp.concatenate([good_f, good_f], axis=1)
    lower = lax.broadcasted_iota(jnp.int32, (1, 128), 1) < 64
    flags = jnp.concatenate(
        [good_2 * jnp.where(lower, keep[2 * t].astype(F32), keep[2 * t + 1].astype(F32)) for t in range(4)], axis=1
    )
    lower8 = lax.broadcasted_iota(jnp.int32, (8, 128), 1) < 64

    def whiten_8(at):
        weight = flags / jnp.maximum(mag[pl.ds(at, 8), :], water)
        re = spec[pl.ds(at, 8), :] * weight
        im = spec[pl.ds(pl.multiple_of(BINS + at, 8), 8), :] * weight
        rows = pl.multiple_of(at * 8, 64)
        for t in range(4):
            r_t, i_t = re[:, 128 * t : 128 * t + 128], im[:, 128 * t : 128 * t + 128]
            turn[pl.ds(rows + 2 * t, 8, stride=8), :] = jnp.where(lower8, r_t, pltpu.roll(i_t, 64, 1))
            turn[pl.ds(rows + 2 * t + 1, 8, stride=8), :] = jnp.where(lower8, pltpu.roll(r_t, 64, 1), i_t)

    def put(at, k, place):
        sent[place] = turn[pl.ds(pl.multiple_of(at * 8 + 8 * k, 8), 8), :].astype(BF16)

    on_0 = core == 0

    @pl.loop(0, 8)
    def _(y0):
        for block in range(3):
            at = pl.multiple_of(y0 * 24 + 8 * block, 8)
            whiten_8(at)
            for k in range(8):
                slot = 8 * block + k
                z0, r0 = slot // 3, slot % 3
                x0 = (r0 + 1 - z0 + 32 - y0) % 4
                place_0 = x0 * 12 + (y0 // 4) * 3 + (z0 * 48 + r0)
                place_1 = y0 * 48 + ((z0 % 2) * 12 + (z0 // 2) * 3 + r0)
                put(at, k, jnp.where(on_0, place_0, place_1))

    if between is not None:
        between()

    @pl.loop(0, 8)
    def _(z1):
        for block in range(3):
            at = pl.multiple_of(192 + z1 * 24 + 8 * block, 8)
            whiten_8(at)
            for k in range(8):
                x1, slot = (8 * block + k) // 6, (8 * block + k) % 6
                yh1, r1 = slot // 3, slot % 3
                yl1 = (r1 + 1 - 2 - x1 + 32 - z1) % 4
                place_0 = z1 * 48 + (x1 * 12 + 6 + slot)
                place_1 = yl1 * 48 + (z1 % 2) * 12 + (z1 // 2) * 3 + (yh1 * 192 + 24 + r1)
                put(at, k, jnp.where(on_0, place_0, place_1))


def gather_blocks(c, got, gram_in):
    for yl in range(4):
        block = got[c, 2 * yl : 2 * yl + 2].astype(F32).reshape(512, 128).astype(BF16)
        gram_in[:, 128 * (4 * c + yl) : 128 * (4 * c + yl) + 128] = block


def block_of(chan):
    return (chan % 2) * 4 + chan // 2


def cross_of(core, chans, gram_in, cross):
    sign = jnp.where(lax.broadcasted_iota(jnp.int32, (1, 128), 1) < 64, 1.0, -1.0).astype(F32)
    b_ids = lax.broadcasted_iota(jnp.int32, (64, 128), 0)
    a_ids = lax.broadcasted_iota(jnp.int32, (64, 128), 1) % 64
    same = b_ids == a_ids
    ids = [block_of(chan) for chan in chans]
    left = jnp.concatenate(
        [gram_in[:, pl.ds(pl.multiple_of(i * 128, 128), 128)] for i in ids], axis=1
    )
    products = lax.dot_general(left, gram_in[...], (((0,), (0,)), ((), ())), preferred_element_type=F32)
    for second in range(2):
        chan_b = chans[second]
        to_y, to_column = (chan_b // 4) * 4, (chan_b % 4) * 8
        base = jnp.where(core == 0, to_column * 16 + to_y * 2, to_y * 64 + turned_column(to_column))
        step_part = jnp.where(core == 0, 16, 1)
        step_row = jnp.where(core == 0, 1, 32)
        for j in range(8):
            tile = products[128 * second : 128 * second + 128, 128 * j : 128 * j + 128]
            summed = tile[:64] + sign * pltpu.roll(tile[64:], 64, 1)
            summed = jnp.where(jnp.logical_and(same, ids[second] == j), 0.0, summed)
            chan_a = (j % 4) * 2 + j // 4
            at = base + step_row * chan_a
            for part in range(8):
                cross[at + step_part * part] = summed[8 * part : 8 * part + 8].astype(BF16)


def make_lhs(z_pair, done_a, done_b, rows_f, lhs_f, lhs_out):
    for quarter in range(4):
        of_pair = (z_pair + 4 - quarter) % 4
        for y in range(8):
            values = done_a[y, 6 * quarter : 6 * quarter + 6].astype(F32).reshape(48, 128)
            rows_f[pl.ds(pl.multiple_of(of_pair * 48 + y * 192, 16), 48), :] = values
    rows_f[1536:3072] = done_b[...].astype(F32).reshape(1536, 128)
    for b in range(8):
        turned = rows_f[pl.ds(b, BINS, stride=8), :].T
        for p in range(2):
            for k in range(3):
                lhs_f[3 * p + k, pl.ds(b, 64, stride=8), :] = turned[64 * p : 64 * p + 64, 128 * k : 128 * k + 128]
    for k in range(6):
        lhs_out[:, 128 * k : 128 * k + 128] = lhs_f[k].astype(BF16)


def stack_kernel(
    wave_hbm, table_hbm, keep_hbm, good_hbm, lhs_out,
    wave, table, keep, good,
    spec, mag, turn, sent, mid_a, mid_b, got, gram_in, cross, back_a, back_b, done_a, done_b, rows_f, lhs_f,
    send_sem, recv_sem, local_sem, load_sem,
):
    chan = lax.axis_index("chan")
    seg = lax.axis_index("seg")
    core = chan % 2
    y = (seg // 32) * 4 + chan // 2
    column = seg % 32
    z, x = column // 4, column % 4
    row = y * 2 + core
    y8 = (chan // 2) * 2 + seg // 32
    owner = share(row, column) != 0

    thirds = [pl.ds(256 * n, 256) for n in range(3)]
    loads = [
        pltpu.make_async_copy(src, dst, load_sem.at[n])
        for n, (src, dst) in enumerate(
            ((wave_hbm, wave), (table_hbm.at[thirds[0]], table.at[thirds[0]]), (keep_hbm, keep), (good_hbm, good),
             (table_hbm.at[thirds[1]], table.at[thirds[1]]), (table_hbm.at[thirds[2]], table.at[thirds[2]]))
        )
    ]
    for load in loads:
        load.start()

    def next_column(k):
        k = 32 - k
        return ((z + ring_8(k % 8)) % 8) * 4 + (x + ring_4(k // 8)) % 4

    def next_row(k):
        k = 16 - k
        return ((y + ring_8(k % 8)) % 8) * 2 + (core + k // 8) % 2

    barrier = pltpu.get_barrier_semaphore()

    @pl.loop(1, 32)
    def _(k):
        pl.semaphore_signal(barrier, inc=1, device_id=device_of(row, next_column(k)), device_id_type=MESH)

    @pl.loop(1, 16)
    def _(k):
        pl.semaphore_signal(barrier, inc=1, device_id=device_of(next_row(k), column), device_id_type=MESH)

    def remote(src, dst, n, m, to_row, to_column):
        return pltpu.make_async_remote_copy(
            src_ref=src, dst_ref=dst, send_sem=send_sem.at[n], recv_sem=recv_sem.at[m],
            device_id=device_of(to_row, to_column), device_id_type=MESH,
        )

    def local(src, dst, n):
        return pltpu.make_async_copy(src, dst, local_sem.at[n])

    def wait_bytes(ref, sem):
        pltpu.make_async_copy(ref, ref, sem).wait()

    def loaded(third):
        for n in ((0, 1, 2, 3), (4,), (5,))[third]:
            loads[n].wait()

    def to_columns(c):
        @pl.loop(1, 32)
        def _(k):
            to = next_column(k)
            remote(sent.at[pl.ds(to * 12 + 6 * c, 6)], mid_a.at[column, pl.ds(6 * c, 6)], 0, c, row, to).start()

    def to_rows(c, to_core):
        @pl.loop(0, 8)
        def _(k):
            to = ((y + ring_8(7 - k)) % 8) * 2 + to_core

            @pl.when(to != row)
            def _():
                remote(sent.at[pl.ds(to * 24 + 12 * c, 12)], mid_b.at[y8, pl.ds(12 * c, 12)], 1, 2 + c, to, column).start()

    def first_sends():
        pl.semaphore_wait(barrier, 46)

        @pl.when(core == 0)
        def _():
            to_columns(0)

        @pl.when(core == 1)
        def _():
            to_rows(0, 0)

    make_units(core, wave, table, keep, good, spec, mag, turn, sent, loaded, first_sends)

    @pl.when(core == 0)
    def _():
        to_columns(1)
        local(sent.at[pl.ds(column * 12, 12)], mid_a.at[column], 0).start()

    @pl.when(core == 1)
    def _():
        to_rows(0, 1)
        to_rows(1, 0)
        to_rows(1, 1)
        local(sent.at[pl.ds(row * 24, 24)], mid_b.at[y8], 1).start()

    @pl.when(core == 0)
    def _():
        wait_bytes(mid_a.at[0], local_sem.at[0])

    @pl.when(core == 1)
    def _():
        wait_bytes(mid_b.at[0], local_sem.at[1])

    for c in range(2):
        @pl.when(core == 0)
        def _():
            wait_bytes(mid_a.at[pl.ds(0, 31), pl.ds(0, 6)], recv_sem.at[c])

            @pl.loop(0, 8)
            def _(k):
                to = ((y + ring_8(7 - k)) % 8) * 2 + c

                @pl.when(jnp.logical_and(share(to, column) != 0, to != row))
                def _():
                    remote(mid_a.at[:, column_slot(to, column)], got.at[0, y8], 2, 4, to, column).start()

            wait_bytes(mid_b.at[:, pl.ds(0, 12)], recv_sem.at[2 + c])

        @pl.when(core == 1)
        def _():
            wait_bytes(mid_b.at[pl.ds(0, 7), pl.ds(0, 12)], recv_sem.at[2 + c])

        @pl.loop(0, 16)
        def _(k):
            back = 15 - k
            to = ((z + (z + c) % 2 + 2 * ring_4(back % 4)) % 8) * 4 + (x + ring_4(back // 4)) % 4

            @pl.when(jnp.logical_and(share(row, to) != 0, to != column))
            def _():
                remote(mid_b.at[:, row_slot_by_parity(row, to)], got.at[1, :, column], 3, 5, row, to).start()

    @pl.when(owner)
    def _():
        @pl.when(core == 0)
        def _():
            local(mid_a.at[:, column_slot(row, column)], got.at[0, y8], 2).start()

        local(mid_b.at[:, row_slot_by_parity(row, column)], got.at[1, :, column], 3).start()
        @pl.when(core == 0)
        def _():
            wait_bytes(got.at[0, 0], local_sem.at[2])
            wait_bytes(got.at[0, pl.ds(0, 7)], recv_sem.at[4])

        @pl.when(core == 1)
        def _():
            wait_bytes(got.at[0], recv_sem.at[4])

        gather_blocks(0, got, gram_in)
        wait_bytes(got.at[1, :, 0], local_sem.at[3])
        wait_bytes(got.at[1, :, pl.ds(0, 31)], recv_sem.at[5])
        gather_blocks(1, got, gram_in)

        slot_a = row_slot(row, column) % 6
        slot_b = column_slot(row, column) % 6

        @pl.loop(0, 4)
        def _(quarter):
            pair = (quarter + z // 2) % 4
            to_hi, half = (quarter // 2 + 1 - y // 4) % 2, quarter % 2
            first = jnp.where(core == 0, pair, to_hi * 4 + half)
            second = jnp.where(core == 0, pair + 4, to_hi * 4 + half + 2)
            cross_of(core, (first, second), gram_in, cross)

            @pl.when(core == 0)
            def _():
                @pl.loop(0, 8)
                def _(k):
                    to = pair * 8 + (column + k + 1) % 8
                    slot = quarter * 6 + slot_a

                    @pl.when(to != column)
                    def _():
                        remote(cross.at[pl.ds(to * 16, 16)], back_a.at[slot], 4, 6 + quarter // 2, row, to).start()

                    @pl.when(to == column)
                    def _():
                        local(cross.at[pl.ds(to * 16, 16)], back_a.at[slot], 4).start()

            @pl.when(core == 1)
            def _():
                @pl.loop(0, 8)
                def _(k):
                    to = to_hi * 8 + (row + k + 1) % 8
                    src = cross.at[pl.ds(to * 32 + half * 16, 16)]
                    dst = back_b.at[slot_b, pl.ds(half * 16, 16)]

                    @pl.when(to != row)
                    def _():
                        remote(src, dst, 5, 8 + half, to, column).start()

                    @pl.when(to == row)
                    def _():
                        local(src, dst, 5).start()

    own_a = jnp.logical_and(owner, core == 0)
    own_b = jnp.logical_and(owner, core == 1)

    @pl.when(own_b)
    def _():
        wait_bytes(back_b.at[0], local_sem.at[5])

    for c in range(2):
        @pl.when(core == 0)
        def _():
            if c == 0:
                @pl.when(own_a)
                def _():
                    wait_bytes(back_a.at[0], local_sem.at[4])
                    wait_bytes(back_a.at[pl.ds(0, 11)], recv_sem.at[6])

                @pl.when(jnp.logical_not(own_a))
                def _():
                    wait_bytes(back_a.at[pl.ds(0, 12)], recv_sem.at[6])
            else:
                wait_bytes(back_a.at[pl.ds(0, 12)], recv_sem.at[7])

            @pl.loop(1, 16)
            def _(k):
                to = next_row(k)
                slots = pl.ds(12 * c, 12)
                remote(back_a.at[slots, to], done_a.at[y, slots], 6, 10, to, column).start()

        @pl.when(own_b)
        def _():
            wait_bytes(back_b.at[pl.ds(0, 5), pl.ds(0, 16)], recv_sem.at[8 + c])

        @pl.when(jnp.logical_not(own_b))
        def _():
            wait_bytes(back_b.at[:, pl.ds(0, 16)], recv_sem.at[8 + c])

        @pl.loop(0, 16)
        def _(k):
            place = (turned_column(column) + k + 1) % 16
            to = (place // 8) * 16 + c * 8 + place % 8

            @pl.when(to != column)
            def _():
                remote(back_b.at[:, place + 16 * c], done_b.at[column], 7, 11, row, to).start()

    @pl.when(core == 0)
    def _():
        local(back_a.at[:, row], done_a.at[y], 6).start()

    local(back_b.at[:, turned_column(column)], done_b.at[column], 7).start()

    @pl.when(core == 0)
    def _():
        wait_bytes(done_a.at[0], local_sem.at[6])
        wait_bytes(done_a.at[pl.ds(0, 7)], recv_sem.at[10])

    @pl.when(core == 1)
    def _():
        wait_bytes(done_a, recv_sem.at[10])

    wait_bytes(done_b.at[0], local_sem.at[7])
    wait_bytes(done_b.at[pl.ds(0, 31)], recv_sem.at[11])
    make_lhs(z // 2, done_a, done_b, rows_f, lhs_f, lhs_out)

    @pl.when(core == 0)
    def _():
        wait_bytes(mid_a.at[pl.ds(0, 31)], send_sem.at[0])

        @pl.when(owner)
        def _():
            wait_bytes(got.at[0, pl.ds(0, 8)], send_sem.at[2])
            wait_bytes(got.at[0, pl.ds(0, 3)], send_sem.at[2])
            wait_bytes(cross.at[pl.ds(0, 31 * 16)], send_sem.at[4])

        @pl.when(jnp.logical_not(owner))
        def _():
            wait_bytes(got.at[0, pl.ds(0, 8)], send_sem.at[2])
            wait_bytes(got.at[0, pl.ds(0, 4)], send_sem.at[2])

        wait_bytes(done_a.at[pl.ds(0, 8)], send_sem.at[6])
        wait_bytes(done_a.at[pl.ds(0, 7)], send_sem.at[6])

    @pl.when(core == 1)
    def _():
        wait_bytes(sent.at[pl.ds(0, 15 * 24)], send_sem.at[1])

        @pl.when(owner)
        def _():
            wait_bytes(cross.at[pl.ds(0, 15 * 32)], send_sem.at[5])

    @pl.when(owner)
    def _():
        wait_bytes(got.at[1, :, pl.ds(0, 23)], send_sem.at[3])

    @pl.when(jnp.logical_not(owner))
    def _():
        wait_bytes(got.at[1, :, pl.ds(0, 24)], send_sem.at[3])

    wait_bytes(done_b.at[pl.ds(0, 31)], send_sem.at[7])


def stacked(wave, table, keep, good):
    in_hbm = pl.BlockSpec(memory_space=pltpu.HBM)
    return pl.pallas_call(
        stack_kernel,
        out_shape=jax.ShapeDtypeStruct((512, 2 * BINS), BF16),
        in_specs=[in_hbm] * 4,
        out_specs=pl.BlockSpec(memory_space=pltpu.VMEM),
        scratch_shapes=[
            pltpu.VMEM((512, NT), BF16),
            pltpu.VMEM((2 * BINS, NT), BF16),
            pltpu.SMEM((8,), jnp.int32),
            pltpu.VMEM((1, 64), jnp.int32),
            pltpu.VMEM((2 * BINS, 512), F32),
            pltpu.VMEM((BINS, 512), F32),
            pltpu.VMEM((BINS * 8, 128), F32),
            pltpu.VMEM((BINS, 8, 128), BF16),
            pltpu.VMEM((32, 12, 8, 128), BF16),
            pltpu.VMEM((8, 24, 8, 128), BF16),
            pltpu.VMEM((2, 8, 32, 8, 128), BF16),
            pltpu.VMEM((512, 1024), BF16),
            pltpu.VMEM((512, 8, 128), BF16),
            pltpu.VMEM((24, 16, 8, 128), BF16),
            pltpu.VMEM((6, 32, 8, 128), BF16),
            pltpu.VMEM((8, 24, 8, 128), BF16),
            pltpu.VMEM((32, 6, 8, 128), BF16),
            pltpu.VMEM((3072, 128), F32),
            pltpu.VMEM((6, 512, 128), F32),
            pltpu.SemaphoreType.DMA((8,)),
            pltpu.SemaphoreType.DMA((12,)),
            pltpu.SemaphoreType.DMA((8,)),
            pltpu.SemaphoreType.DMA((6,)),
        ],
        compiler_params=pltpu.CompilerParams(collective_id=0, has_side_effects=True, vmem_limit_bytes=48 << 20),
        name="stack_cross_spectra",
    )(*[pltpu.with_memory_space_constraint(value, pltpu.HBM) for value in (wave, table, keep, good)])


def lag_kernel(scale, lhs, table, out, block, sem):
    width = block.shape[-1]
    count = LAGS // width
    for n in range(count):
        if n >= 2:
            pltpu.make_async_copy(block.at[n % 2], out.at[:, :, pl.ds((n - 2) * width, width)], sem.at[n % 2]).wait()
        values = jnp.dot(lhs[...], table[:, n * width : (n + 1) * width], preferred_element_type=F32) * scale
        block[n % 2] = values.reshape(64, 8, width).astype(BF16)
        pltpu.make_async_copy(block.at[n % 2], out.at[:, :, pl.ds(n * width, width)], sem.at[n % 2]).start()
    for n in range(count - 2, count):
        pltpu.make_async_copy(block.at[n % 2], out.at[:, :, pl.ds(n * width, width)], sem.at[n % 2]).wait()


def lagged(lhs, table, scale):
    vmem = pl.BlockSpec(memory_space=pltpu.VMEM)
    return pl.pallas_call(
        functools.partial(lag_kernel, scale),
        out_shape=jax.ShapeDtypeStruct((64, 8, LAGS), BF16),
        in_specs=[vmem, vmem],
        out_specs=pl.BlockSpec(memory_space=pl.ANY),
        scratch_shapes=[pltpu.VMEM((2, 64, 8, LAGS // 2), BF16), pltpu.SemaphoreType.DMA((2,))],
        compiler_params=pltpu.CompilerParams(vmem_limit_bytes=48 << 20),
        name="lag_transform",
    )(lhs, table)


def local(waveforms, segment_keep, channel_good):
    wave = waveforms.reshape(512, NT)
    lhs = stacked(wave, jnp.asarray(forward_rows()), segment_keep, channel_good.reshape(1, 64))
    return lagged(lhs, jnp.asarray(lag_rows()), float(1.0 / np.sqrt(SEGS * BINS)))


def solution(mesh):
    placed = (P("seg", "chan", None), P("seg"), P("chan"))
    return jax.shard_map(
        local, mesh=mesh, in_specs=placed, out_specs=P("chan", "seg", None), check_vma=False
    )
```

```python
import functools

import jax
import jax.numpy as jnp
import ml_dtypes
import numpy as np
from jax import lax
from jax.experimental import pallas as pl
from jax.experimental.pallas import tpu as pltpu
from jax.sharding import PartitionSpec as P

NT = 1536
BINS = 384
LOWEST = 12
LAGS = 2560
SEGS = 512
MESH = pl.DeviceIdType.MESH
F32 = jnp.float32
BF16 = jnp.bfloat16


def forward_rows():
    t = np.arange(NT, dtype=np.int64)
    f = LOWEST + np.arange(BINS, dtype=np.int64)
    theta = np.float32(2.0 * np.pi / (2 * NT)) * ((f[:, None] * t[None, :]) % (2 * NT)).astype(np.float32)
    theta = theta.astype(np.float64)
    rows = np.concatenate([np.cos(theta), -np.sin(theta)], axis=0) / np.sqrt(NT)
    return rows.astype(np.float32).astype(ml_dtypes.bfloat16)


def lag_rows():
    f = LOWEST + np.arange(BINS, dtype=np.int64)
    l = np.arange(LAGS, dtype=np.int64) - LAGS // 2
    phi = np.float32(2.0 * np.pi / (2 * NT)) * ((f[:, None] * l[None, :]) % (2 * NT)).astype(np.float32)
    phi = phi.astype(np.float64)
    rows = np.concatenate([np.cos(phi), -np.sin(phi)], axis=0)
    return rows.astype(np.float32).astype(ml_dtypes.bfloat16)


def device_of(row, column):
    y, core = row // 2, row % 2
    return ((y % 4) * 2 + core, (y // 4) * 32 + column)


def share(row, column):
    return (row // 2 + 2 * (row % 2) + column // 4 + column % 4) % 4


def column_slot(row, column):
    return (row % 2) * 6 + (row // 8) * 3 + share(row, column) - 1


def row_slot(row, column):
    return (column // 4) * 3 + share(row, column) - 1


def turned_column(column):
    return ((column // 8) % 2) * 16 + (column // 16) * 8 + column % 8


QUARTERS = (2, 1, 3, 0)


def quarter_of(step):
    return jnp.where(step == 0, 2, jnp.where(step == 1, 1, jnp.where(step == 2, 3, 0)))


def ring_8(k):
    return jnp.where(k % 2 == 1, (k + 1) // 2, (8 - k // 2) % 8)


def ring_4(k):
    return jnp.where(k == 2, 3, jnp.where(k == 3, 2, k))


def make_units(core, wave, table, keep, good, spec, mag, turn, sent, loaded=None, between=None):
    for third in range(3):
        if loaded is not None:
            loaded(third)
        rows = slice(256 * third, 256 * third + 256)
        spec[rows, :] = lax.dot_general(
            table[rows, :], wave[...], (((1,), (1,)), ((), ())), preferred_element_type=F32
        )

    def add_magnitude(g, total):
        at = pl.multiple_of(g * 8, 8)
        re = spec[pl.ds(at, 8), :]
        im = spec[pl.ds(pl.multiple_of(BINS + at, 8), 8), :]
        m = jnp.sqrt(re * re + im * im)
        mag[pl.ds(at, 8), :] = m
        return total + m

    total = lax.fori_loop(0, BINS // 8, add_magnitude, jnp.zeros((8, 512), F32), unroll=4)
    water = 0.5 * (jnp.sum(total, axis=0, keepdims=True) * (1.0 / BINS)) + 1e-06
    good_f = good[...].astype(F32)
    good_2 = jnp.concatenate([good_f, good_f], axis=1)
    lower = lax.broadcasted_iota(jnp.int32, (1, 128), 1) < 64
    flags = jnp.concatenate(
        [good_2 * jnp.where(lower, keep[2 * t].astype(F32), keep[2 * t + 1].astype(F32)) for t in range(4)], axis=1
    )
    lower8 = lax.broadcasted_iota(jnp.int32, (8, 128), 1) < 64

    def whiten_8(at):
        weight = flags / jnp.maximum(mag[pl.ds(at, 8), :], water)
        re = spec[pl.ds(at, 8), :] * weight
        im = spec[pl.ds(BINS + at, 8), :] * weight
        rows = at * 8
        for t in range(4):
            r_t, i_t = re[:, 128 * t : 128 * t + 128], im[:, 128 * t : 128 * t + 128]
            turn[pl.ds(rows + 2 * t, 8, stride=8), :] = jnp.where(lower8, r_t, pltpu.roll(i_t, 64, 1))
            turn[pl.ds(rows + 2 * t + 1, 8, stride=8), :] = jnp.where(lower8, pltpu.roll(r_t, 64, 1), i_t)

    def whiten_half(half):
        for block in range(24):
            whiten_8(half * 192 + 8 * block)

    def place_24(at, places):
        for k, place in enumerate(places):
            sent[place] = turn[pl.ds(pl.multiple_of(at * 8 + 8 * k, 8), 8), :].astype(BF16)

    whiten_half(0)

    @pl.when(core == 0)
    def _():
        @pl.loop(0, 8)
        def _(y0):
            x_base = [((c + 32 - y0) % 4) * 12 + (y0 // 4) * 3 for c in range(4)]
            places = []
            for slot in range(24):
                z0, r0 = slot // 3, slot % 3
                places.append(x_base[(r0 + 1 - z0) % 4] + (z0 * 48 + r0))
            place_24(pl.multiple_of(y0 * 24, 8), places)

    @pl.when(core == 1)
    def _():
        @pl.loop(0, 8)
        def _(y0):
            places = []
            for slot in range(24):
                places.append(y0 * 48 + slot)
            place_24(pl.multiple_of(y0 * 24, 8), places)

    if between is not None:
        between()

    whiten_half(1)

    @pl.when(core == 0)
    def _():
        @pl.loop(0, 8)
        def _(z1):
            places = []
            for n in range(24):
                x1, slot = n // 6, n % 6
                places.append(z1 * 48 + (x1 * 12 + 6 + slot))
            place_24(pl.multiple_of(192 + z1 * 24, 8), places)

    @pl.when(core == 1)
    def _():
        @pl.loop(0, 8)
        def _(z1):
            y_base = [((c + 32 - z1) % 4) * 48 + z1 * 3 for c in range(4)]
            places = []
            for n in range(24):
                x1, slot = n // 6, n % 6
                yh1, r1 = slot // 3, slot % 3
                places.append(y_base[(r1 + 1 - 2 - x1) % 4] + (yh1 * 192 + 24 + r1))
            place_24(pl.multiple_of(192 + z1 * 24, 8), places)


def gather_blocks(c, got, gram_in):
    for yl in range(4):
        block = got[c, 2 * yl : 2 * yl + 2].astype(F32).reshape(512, 128).astype(BF16)
        gram_in[:, 128 * (4 * c + yl) : 128 * (4 * c + yl) + 128] = block


def block_of(chan):
    return (chan % 2) * 4 + chan // 2


def cross_of(core, chans, gram_in, cross):
    sign = jnp.where(lax.broadcasted_iota(jnp.int32, (1, 128), 1) < 64, 1.0, -1.0).astype(F32)
    b_ids = lax.broadcasted_iota(jnp.int32, (64, 128), 0)
    a_ids = lax.broadcasted_iota(jnp.int32, (64, 128), 1) % 64
    same = b_ids == a_ids
    ids = [block_of(chan) for chan in chans]
    left = jnp.concatenate(
        [gram_in[:, pl.ds(pl.multiple_of(i * 128, 128), 128)] for i in ids], axis=1
    )
    products = lax.dot_general(left, gram_in[...], (((0,), (0,)), ((), ())), preferred_element_type=F32)
    for second in range(2):
        chan_b = chans[second]
        to_y, to_column = (chan_b // 4) * 4, (chan_b % 4) * 8
        base = jnp.where(core == 0, to_column * 16 + to_y * 2, to_y * 64 + turned_column(to_column))
        step_part = jnp.where(core == 0, 16, 1)
        step_row = jnp.where(core == 0, 1, 32)
        for j in range(8):
            tile = products[128 * second : 128 * second + 128, 128 * j : 128 * j + 128]
            summed = tile[:64] + sign * pltpu.roll(tile[64:], 64, 1)
            summed = jnp.where(jnp.logical_and(same, ids[second] == j), 0.0, summed)
            chan_a = (j % 4) * 2 + j // 4
            at = base + step_row * chan_a
            for part in range(8):
                cross[at + step_part * part] = summed[8 * part : 8 * part + 8].astype(BF16)


def make_lhs(z_pair, done_a, done_b, rows_f, lhs_f, lhs_out):
    for step in range(4):
        of_pair = (z_pair + 4 - QUARTERS[step]) % 4
        for y in range(8):
            values = done_a[y, 6 * step : 6 * step + 6].astype(F32).reshape(48, 128)
            rows_f[pl.ds(pl.multiple_of(of_pair * 48 + y * 192, 16), 48), :] = values
    rows_f[1536:3072] = done_b[...].astype(F32).reshape(1536, 128)
    for b in range(8):
        turned = rows_f[pl.ds(b, BINS, stride=8), :].T
        for p in range(2):
            for k in range(3):
                lhs_f[3 * p + k, pl.ds(b, 64, stride=8), :] = turned[64 * p : 64 * p + 64, 128 * k : 128 * k + 128]
    for k in range(6):
        lhs_out[:, 128 * k : 128 * k + 128] = lhs_f[k].astype(BF16)


def stack_kernel(
    wave_hbm, table_hbm, keep_hbm, good_hbm, lag_hbm, lhs_out, lag_out,
    wave, table, keep, good,
    spec, mag, turn, sent, mid_a, mid_b, got, gram_in, cross, back_a, back_b, done_a, done_b, rows_f, lhs_f,
    send_sem, recv_sem, local_sem, load_sem,
):
    chan = lax.axis_index("chan")
    seg = lax.axis_index("seg")
    core = chan % 2
    y = (seg // 32) * 4 + chan // 2
    column = seg % 32
    z, x = column // 4, column % 4
    row = y * 2 + core
    y8 = (chan // 2) * 2 + seg // 32
    owner = share(row, column) != 0

    thirds = [pl.ds(256 * n, 256) for n in range(3)]
    loads = [
        pltpu.make_async_copy(src, dst, load_sem.at[n])
        for n, (src, dst) in enumerate(
            ((wave_hbm, wave), (table_hbm.at[thirds[0]], table.at[thirds[0]]), (keep_hbm, keep), (good_hbm, good),
             (table_hbm.at[thirds[1]], table.at[thirds[1]]), (table_hbm.at[thirds[2]], table.at[thirds[2]]))
        )
    ]
    for load in loads:
        load.start()

    def next_column(k):
        k = 32 - k
        return ((z + ring_8(k % 8)) % 8) * 4 + (x + ring_4(k // 8)) % 4

    def next_row(k):
        k = 16 - k
        return ((y + ring_8(k % 8)) % 8) * 2 + (core + k // 8) % 2

    barrier = pltpu.get_barrier_semaphore()

    @pl.loop(1, 32)
    def _(k):
        pl.semaphore_signal(barrier, inc=1, device_id=device_of(row, next_column(k)), device_id_type=MESH)

    @pl.loop(1, 16)
    def _(k):
        pl.semaphore_signal(barrier, inc=1, device_id=device_of(next_row(k), column), device_id_type=MESH)

    def remote(src, dst, n, m, to_row, to_column):
        return pltpu.make_async_remote_copy(
            src_ref=src, dst_ref=dst, send_sem=send_sem.at[n], recv_sem=recv_sem.at[m],
            device_id=device_of(to_row, to_column), device_id_type=MESH,
        )

    def local(src, dst, n):
        return pltpu.make_async_copy(src, dst, local_sem.at[n])

    def wait_bytes(ref, sem):
        pltpu.make_async_copy(ref, ref, sem).wait()

    def loaded(third):
        for n in ((0, 1, 2, 3), (4,), (5,))[third]:
            loads[n].wait()

    def to_columns(c):
        @pl.loop(1, 32)
        def _(k):
            to = next_column(k)
            remote(sent.at[pl.ds(to * 12 + 6 * c, 6)], mid_a.at[column, pl.ds(6 * c, 6)], 0, c, row, to).start()

    def to_rows(to_core):
        @pl.loop(0, 8)
        def _(k):
            to = ((y + ring_8(7 - k)) % 8) * 2 + to_core

            @pl.when(to != row)
            def _():
                remote(sent.at[pl.ds(to * 24, 24)], mid_b.at[y8], 1, 2, to, column).start()

    def first_sends():
        pltpu.make_async_copy(lag_hbm, lag_out, load_sem.at[6]).start()
        pl.semaphore_wait(barrier, 46)

        @pl.when(core == 0)
        def _():
            to_columns(0)

        @pl.when(core == 1)
        def _():
            to_rows(0)

    make_units(core, wave, table, keep, good, spec, mag, turn, sent, loaded, first_sends)

    @pl.when(core == 0)
    def _():
        to_columns(1)
        local(sent.at[pl.ds(column * 12, 12)], mid_a.at[column], 0).start()

    @pl.when(core == 1)
    def _():
        to_rows(1)
        local(sent.at[pl.ds(row * 24, 24)], mid_b.at[y8], 1).start()

    def to_owners_in_column(to_core):
        @pl.loop(0, 8)
        def _(k):
            to = ((y + ring_8(7 - k)) % 8) * 2 + to_core

            @pl.when(jnp.logical_and(share(to, column) != 0, to != row))
            def _():
                remote(mid_a.at[:, column_slot(to, column)], got.at[0, y8], 2, 4, to, column).start()

    def to_owners_in_row():
        @pl.loop(1, 32)
        def _(k):
            to = next_column(k)

            @pl.when(share(row, to) != 0)
            def _():
                remote(mid_b.at[:, row_slot(row, to)], got.at[1, :, column], 3, 5, row, to).start()

    @pl.when(core == 0)
    def _():
        wait_bytes(mid_a.at[0], local_sem.at[0])
        wait_bytes(mid_a.at[pl.ds(0, 31), pl.ds(0, 6)], recv_sem.at[0])
        to_owners_in_column(0)
        wait_bytes(mid_b, recv_sem.at[2])
        to_owners_in_row()
        wait_bytes(mid_a.at[pl.ds(0, 31), pl.ds(0, 6)], recv_sem.at[1])
        to_owners_in_column(1)

    @pl.when(core == 1)
    def _():
        wait_bytes(mid_b.at[0], local_sem.at[1])
        wait_bytes(mid_b.at[pl.ds(0, 7)], recv_sem.at[2])
        to_owners_in_row()

    @pl.when(owner)
    def _():
        @pl.when(core == 0)
        def _():
            local(mid_a.at[:, column_slot(row, column)], got.at[0, y8], 2).start()

        local(mid_b.at[:, row_slot(row, column)], got.at[1, :, column], 3).start()
        @pl.when(core == 0)
        def _():
            wait_bytes(got.at[0, 0], local_sem.at[2])
            wait_bytes(got.at[0, pl.ds(0, 7)], recv_sem.at[4])

        @pl.when(core == 1)
        def _():
            wait_bytes(got.at[0], recv_sem.at[4])

        gather_blocks(0, got, gram_in)
        wait_bytes(got.at[1, :, 0], local_sem.at[3])
        wait_bytes(got.at[1, :, pl.ds(0, 31)], recv_sem.at[5])
        gather_blocks(1, got, gram_in)

        slot_a = row_slot(row, column) % 6
        slot_b = column_slot(row, column) % 6

        @pl.loop(0, 4)
        def _(step):
            pair = (quarter_of(step) + z // 2) % 4
            to_hi, half = (step // 2 + 1 - y // 4) % 2, step % 2
            first = jnp.where(core == 0, pair, to_hi * 4 + half)
            second = jnp.where(core == 0, pair + 4, to_hi * 4 + half + 2)
            cross_of(core, (first, second), gram_in, cross)

            @pl.when(core == 0)
            def _():
                @pl.loop(0, 8)
                def _(k):
                    to = pair * 8 + (column + k + 1) % 8
                    slot = step * 6 + slot_a

                    @pl.when(to != column)
                    def _():
                        remote(cross.at[pl.ds(to * 16, 16)], back_a.at[slot], 4, 6 + step // 2, row, to).start()

                    @pl.when(to == column)
                    def _():
                        local(cross.at[pl.ds(to * 16, 16)], back_a.at[slot], 4).start()

            @pl.when(core == 1)
            def _():
                @pl.loop(0, 8)
                def _(k):
                    to = to_hi * 8 + (row + k + 1) % 8
                    src = cross.at[pl.ds(to * 32 + half * 16, 16)]
                    dst = back_b.at[slot_b, pl.ds(half * 16, 16)]

                    @pl.when(to != row)
                    def _():
                        remote(src, dst, 5, 8 + half, to, column).start()

                    @pl.when(to == row)
                    def _():
                        local(src, dst, 5).start()

    own_a = jnp.logical_and(owner, core == 0)
    own_b = jnp.logical_and(owner, core == 1)

    @pl.when(own_b)
    def _():
        wait_bytes(back_b.at[0], local_sem.at[5])

    @pl.when(core == 0)
    def _():
        for c in range(2):
            if c == 1:
                @pl.when(own_a)
                def _():
                    wait_bytes(back_a.at[0], local_sem.at[4])
                    wait_bytes(back_a.at[pl.ds(0, 11)], recv_sem.at[7])

                @pl.when(jnp.logical_not(own_a))
                def _():
                    wait_bytes(back_a.at[pl.ds(0, 12)], recv_sem.at[7])
            else:
                wait_bytes(back_a.at[pl.ds(0, 12)], recv_sem.at[6])

            @pl.loop(1, 16)
            def _(k):
                to = next_row(k)
                slots = pl.ds(12 * c, 12)
                remote(back_a.at[slots, to], done_a.at[y, slots], 6, 10, to, column).start()

    for c in range(2):
        @pl.when(own_b)
        def _():
            wait_bytes(back_b.at[pl.ds(0, 5), pl.ds(0, 16)], recv_sem.at[8 + c])

        @pl.when(jnp.logical_not(own_b))
        def _():
            wait_bytes(back_b.at[:, pl.ds(0, 16)], recv_sem.at[8 + c])

        @pl.loop(0, 16)
        def _(k):
            place = (turned_column(column) + k + 1) % 16
            to = (place // 8) * 16 + c * 8 + place % 8

            @pl.when(to != column)
            def _():
                remote(back_b.at[:, place + 16 * c], done_b.at[column], 7, 11, row, to).start()

    @pl.when(core == 0)
    def _():
        local(back_a.at[:, row], done_a.at[y], 6).start()

    local(back_b.at[:, turned_column(column)], done_b.at[column], 7).start()

    @pl.when(core == 0)
    def _():
        wait_bytes(done_a.at[0], local_sem.at[6])
        wait_bytes(done_a.at[pl.ds(0, 7)], recv_sem.at[10])

    @pl.when(core == 1)
    def _():
        wait_bytes(done_a, recv_sem.at[10])

    wait_bytes(done_b.at[0], local_sem.at[7])
    wait_bytes(done_b.at[pl.ds(0, 31)], recv_sem.at[11])
    make_lhs(z // 2, done_a, done_b, rows_f, lhs_f, lhs_out)

    pltpu.make_async_copy(lag_hbm, lag_out, load_sem.at[6]).wait()

    @pl.when(core == 0)
    def _():
        wait_bytes(mid_a.at[pl.ds(0, 31)], send_sem.at[0])

        @pl.when(owner)
        def _():
            wait_bytes(got.at[0, pl.ds(0, 8)], send_sem.at[2])
            wait_bytes(got.at[0, pl.ds(0, 3)], send_sem.at[2])
            wait_bytes(cross.at[pl.ds(0, 31 * 16)], send_sem.at[4])

        @pl.when(jnp.logical_not(owner))
        def _():
            wait_bytes(got.at[0, pl.ds(0, 8)], send_sem.at[2])
            wait_bytes(got.at[0, pl.ds(0, 4)], send_sem.at[2])

        wait_bytes(done_a.at[pl.ds(0, 8)], send_sem.at[6])
        wait_bytes(done_a.at[pl.ds(0, 7)], send_sem.at[6])

    @pl.when(core == 1)
    def _():
        wait_bytes(sent.at[pl.ds(0, 15 * 24)], send_sem.at[1])

        @pl.when(owner)
        def _():
            wait_bytes(cross.at[pl.ds(0, 15 * 32)], send_sem.at[5])

    @pl.when(owner)
    def _():
        wait_bytes(got.at[1, :, pl.ds(0, 23)], send_sem.at[3])

    @pl.when(jnp.logical_not(owner))
    def _():
        wait_bytes(got.at[1, :, pl.ds(0, 24)], send_sem.at[3])

    wait_bytes(done_b.at[pl.ds(0, 31)], send_sem.at[7])


def stacked(wave, table, keep, good, lag):
    in_hbm = pl.BlockSpec(memory_space=pltpu.HBM)
    return pl.pallas_call(
        stack_kernel,
        out_shape=(pltpu.VMEM((512, 2 * BINS), BF16), pltpu.VMEM((2 * BINS, LAGS), BF16)),
        in_specs=[in_hbm] * 5,
        out_specs=(pl.BlockSpec(memory_space=pltpu.VMEM),) * 2,
        scratch_shapes=[
            pltpu.VMEM((512, NT), BF16),
            pltpu.VMEM((2 * BINS, NT), BF16),
            pltpu.SMEM((8,), jnp.int32),
            pltpu.VMEM((1, 64), jnp.int32),
            pltpu.VMEM((2 * BINS, 512), F32),
            pltpu.VMEM((BINS, 512), F32),
            pltpu.VMEM((BINS * 8, 128), F32),
            pltpu.VMEM((BINS, 8, 128), BF16),
            pltpu.VMEM((32, 12, 8, 128), BF16),
            pltpu.VMEM((8, 24, 8, 128), BF16),
            pltpu.VMEM((2, 8, 32, 8, 128), BF16),
            pltpu.VMEM((512, 1024), BF16),
            pltpu.VMEM((512, 8, 128), BF16),
            pltpu.VMEM((24, 16, 8, 128), BF16),
            pltpu.VMEM((6, 32, 8, 128), BF16),
            pltpu.VMEM((8, 24, 8, 128), BF16),
            pltpu.VMEM((32, 6, 8, 128), BF16),
            pltpu.VMEM((3072, 128), F32),
            pltpu.VMEM((6, 512, 128), F32),
            pltpu.SemaphoreType.DMA((8,)),
            pltpu.SemaphoreType.DMA((12,)),
            pltpu.SemaphoreType.DMA((8,)),
            pltpu.SemaphoreType.DMA((7,)),
        ],
        compiler_params=pltpu.CompilerParams(collective_id=0, has_side_effects=True, vmem_limit_bytes=48 << 20),
        name="stack_cross_spectra",
    )(*[pltpu.with_memory_space_constraint(value, pltpu.HBM) for value in (wave, table, keep, good, lag)])


def lag_kernel(scale, lhs, table, out, block, sem):
    width = block.shape[-1]
    count = LAGS // width
    for n in range(count):
        if n >= 2:
            pltpu.make_async_copy(block.at[n % 2], out.at[:, :, pl.ds((n - 2) * width, width)], sem.at[n % 2]).wait()
        values = jnp.dot(lhs[...], table[:, n * width : (n + 1) * width], preferred_element_type=F32) * scale
        block[n % 2] = values.reshape(64, 8, width).astype(BF16)
        pltpu.make_async_copy(block.at[n % 2], out.at[:, :, pl.ds(n * width, width)], sem.at[n % 2]).start()
    for n in range(count - 2, count):
        pltpu.make_async_copy(block.at[n % 2], out.at[:, :, pl.ds(n * width, width)], sem.at[n % 2]).wait()


def lagged(lhs, table, scale):
    vmem = pl.BlockSpec(memory_space=pltpu.VMEM)
    return pl.pallas_call(
        functools.partial(lag_kernel, scale),
        out_shape=jax.ShapeDtypeStruct((64, 8, LAGS), BF16),
        in_specs=[vmem, vmem],
        out_specs=pl.BlockSpec(memory_space=pl.ANY),
        scratch_shapes=[pltpu.VMEM((2, 64, 8, LAGS // 2), BF16), pltpu.SemaphoreType.DMA((2,))],
        compiler_params=pltpu.CompilerParams(vmem_limit_bytes=48 << 20),
        name="lag_transform",
    )(lhs, table)


def local(waveforms, segment_keep, channel_good):
    wave = waveforms.reshape(512, NT)
    lhs, lag = stacked(
        wave, jnp.asarray(forward_rows()), segment_keep, channel_good.reshape(1, 64), jnp.asarray(lag_rows())
    )
    return lagged(lhs, lag, float(1.0 / np.sqrt(SEGS * BINS)))


def solution(mesh):
    placed = (P("seg", "chan", None), P("seg"), P("chan"))
    return jax.shard_map(
        local, mesh=mesh, in_specs=placed, out_specs=P("chan", "seg", None), check_vma=False
    )
```

```python
import functools

import jax
import jax.numpy as jnp
import ml_dtypes
import numpy as np
from jax import lax
from jax.experimental import pallas as pl
from jax.experimental.pallas import tpu as pltpu
from jax.sharding import PartitionSpec as P

NT = 1536
BINS = 384
LOWEST = 12
LAGS = 2560
SEGS = 512
MESH = pl.DeviceIdType.MESH
F32 = jnp.float32
BF16 = jnp.bfloat16


def forward_rows():
    t = np.arange(NT, dtype=np.int64)
    f = LOWEST + np.arange(BINS, dtype=np.int64)
    theta = np.float32(2.0 * np.pi / (2 * NT)) * ((f[:, None] * t[None, :]) % (2 * NT)).astype(np.float32)
    theta = theta.astype(np.float64)
    rows = np.concatenate([np.cos(theta), -np.sin(theta)], axis=0) / np.sqrt(NT)
    return rows.astype(np.float32).astype(ml_dtypes.bfloat16)


def lag_rows():
    f = LOWEST + np.arange(BINS, dtype=np.int64)
    l = np.arange(LAGS, dtype=np.int64) - LAGS // 2
    phi = np.float32(2.0 * np.pi / (2 * NT)) * ((f[:, None] * l[None, :]) % (2 * NT)).astype(np.float32)
    phi = phi.astype(np.float64)
    rows = np.concatenate([np.cos(phi), -np.sin(phi)], axis=0)
    return rows.astype(np.float32).astype(ml_dtypes.bfloat16)


def device_of(row, column):
    y, core = row // 2, row % 2
    return ((y % 4) * 2 + core, (y // 4) * 32 + column)


def share(row, column):
    return (row // 2 + 2 * (row % 2) + column // 4 + column % 4) % 4


def column_slot(row, column):
    return (row % 2) * 6 + (row // 8) * 3 + share(row, column) - 1


def row_slot(row, column):
    return (column // 4) * 3 + share(row, column) - 1


def turned_column(column):
    return ((column // 8) % 2) * 16 + (column // 16) * 8 + column % 8


QUARTERS = (2, 1, 3, 0)


def quarter_of(step):
    return jnp.where(step == 0, 2, jnp.where(step == 1, 1, jnp.where(step == 2, 3, 0)))


def ring_8(k):
    return jnp.where(k % 2 == 1, (k + 1) // 2, (8 - k // 2) % 8)


def ring_4(k):
    return jnp.where(k == 2, 3, jnp.where(k == 3, 2, k))


def make_units(core, wave, table, keep, good, spec, mag, turn, sent, loaded=None, between=None):
    for third in range(3):
        if loaded is not None:
            loaded(third)
        rows = slice(256 * third, 256 * third + 256)
        spec[rows, :] = lax.dot_general(
            table[rows, :], wave[...], (((1,), (1,)), ((), ())), preferred_element_type=F32
        )

    def add_magnitude(g, total):
        at = pl.multiple_of(g * 8, 8)
        re = spec[pl.ds(at, 8), :]
        im = spec[pl.ds(pl.multiple_of(BINS + at, 8), 8), :]
        m = jnp.sqrt(re * re + im * im)
        mag[pl.ds(at, 8), :] = m
        return total + m

    total = lax.fori_loop(0, BINS // 8, add_magnitude, jnp.zeros((8, 512), F32), unroll=4)
    water = 0.5 * (jnp.sum(total, axis=0, keepdims=True) * (1.0 / BINS)) + 1e-06
    good_f = good[...].astype(F32)
    good_2 = jnp.concatenate([good_f, good_f], axis=1)
    lower = lax.broadcasted_iota(jnp.int32, (1, 128), 1) < 64
    flags = jnp.concatenate(
        [good_2 * jnp.where(lower, keep[2 * t].astype(F32), keep[2 * t + 1].astype(F32)) for t in range(4)], axis=1
    )
    lower8 = lax.broadcasted_iota(jnp.int32, (8, 128), 1) < 64

    def whiten_8(at):
        weight = flags / jnp.maximum(mag[pl.ds(at, 8), :], water)
        re = spec[pl.ds(at, 8), :] * weight
        im = spec[pl.ds(BINS + at, 8), :] * weight
        rows = at * 8
        for t in range(4):
            r_t, i_t = re[:, 128 * t : 128 * t + 128], im[:, 128 * t : 128 * t + 128]
            turn[pl.ds(rows + 2 * t, 8, stride=8), :] = jnp.where(lower8, r_t, pltpu.roll(i_t, 64, 1))
            turn[pl.ds(rows + 2 * t + 1, 8, stride=8), :] = jnp.where(lower8, pltpu.roll(r_t, 64, 1), i_t)

    def whiten_half(half):
        for block in range(24):
            whiten_8(half * 192 + 8 * block)

    def place_24(at, places):
        for k, place in enumerate(places):
            sent[place] = turn[pl.ds(pl.multiple_of(at * 8 + 8 * k, 8), 8), :].astype(BF16)

    whiten_half(0)

    @pl.when(core == 0)
    def _():
        @pl.loop(0, 8)
        def _(y0):
            x_base = [((c + 32 - y0) % 4) * 12 + (y0 // 4) * 3 for c in range(4)]
            places = []
            for slot in range(24):
                z0, r0 = slot // 3, slot % 3
                places.append(x_base[(r0 + 1 - z0) % 4] + (z0 * 48 + r0))
            place_24(pl.multiple_of(y0 * 24, 8), places)

    @pl.when(core == 1)
    def _():
        @pl.loop(0, 8)
        def _(y0):
            places = []
            for slot in range(24):
                places.append(y0 * 48 + slot)
            place_24(pl.multiple_of(y0 * 24, 8), places)

    if between is not None:
        between()

    whiten_half(1)

    @pl.when(core == 0)
    def _():
        @pl.loop(0, 8)
        def _(z1):
            places = []
            for n in range(24):
                x1, slot = n // 6, n % 6
                places.append(z1 * 48 + (x1 * 12 + 6 + slot))
            place_24(pl.multiple_of(192 + z1 * 24, 8), places)

    @pl.when(core == 1)
    def _():
        @pl.loop(0, 8)
        def _(z1):
            y_base = [((c + 32 - z1) % 4) * 48 + z1 * 3 for c in range(4)]
            places = []
            for n in range(24):
                x1, slot = n // 6, n % 6
                yh1, r1 = slot // 3, slot % 3
                places.append(y_base[(r1 + 1 - 2 - x1) % 4] + (yh1 * 192 + 24 + r1))
            place_24(pl.multiple_of(192 + z1 * 24, 8), places)


def gather_blocks(c, got, gram_in):
    for yl in range(4):
        block = got[c, 2 * yl : 2 * yl + 2].astype(F32).reshape(512, 128).astype(BF16)
        gram_in[:, 128 * (4 * c + yl) : 128 * (4 * c + yl) + 128] = block


def block_of(chan):
    return (chan % 2) * 4 + chan // 2


def cross_of(core, chans, gram_in, cross):
    sign = jnp.where(lax.broadcasted_iota(jnp.int32, (1, 128), 1) < 64, 1.0, -1.0).astype(F32)
    b_ids = lax.broadcasted_iota(jnp.int32, (64, 128), 0)
    a_ids = lax.broadcasted_iota(jnp.int32, (64, 128), 1) % 64
    same = b_ids == a_ids
    ids = [block_of(chan) for chan in chans]
    left = jnp.concatenate(
        [gram_in[:, pl.ds(pl.multiple_of(i * 128, 128), 128)] for i in ids], axis=1
    )
    products = lax.dot_general(left, gram_in[...], (((0,), (0,)), ((), ())), preferred_element_type=F32)
    for second in range(2):
        chan_b = chans[second]
        to_y, to_column = (chan_b // 4) * 4, (chan_b % 4) * 8
        base = jnp.where(core == 0, to_column * 16 + to_y * 2, to_y * 64 + turned_column(to_column))
        step_part = jnp.where(core == 0, 16, 1)
        step_row = jnp.where(core == 0, 1, 32)
        for j in range(8):
            tile = products[128 * second : 128 * second + 128, 128 * j : 128 * j + 128]
            summed = tile[:64] + sign * pltpu.roll(tile[64:], 64, 1)
            summed = jnp.where(jnp.logical_and(same, ids[second] == j), 0.0, summed)
            chan_a = (j % 4) * 2 + j // 4
            at = base + step_row * chan_a
            for part in range(8):
                cross[at + step_part * part] = summed[8 * part : 8 * part + 8].astype(BF16)


def make_lhs(z_pair, done_a, done_b, rows_f, lhs_f, lhs_out):
    for step in range(4):
        of_pair = (z_pair + 4 - QUARTERS[step]) % 4
        for y in range(8):
            values = done_a[y, 6 * step : 6 * step + 6].astype(F32).reshape(48, 128)
            rows_f[pl.ds(pl.multiple_of(of_pair * 48 + y * 192, 16), 48), :] = values
    rows_f[1536:3072] = done_b[...].astype(F32).reshape(1536, 128)
    for b in range(8):
        turned = rows_f[pl.ds(b, BINS, stride=8), :].T
        for p in range(2):
            for k in range(3):
                lhs_f[3 * p + k, pl.ds(b, 64, stride=8), :] = turned[64 * p : 64 * p + 64, 128 * k : 128 * k + 128]
    for k in range(6):
        lhs_out[:, 128 * k : 128 * k + 128] = lhs_f[k].astype(BF16)


def stack_kernel(
    wave_hbm, table_hbm, keep_hbm, good_hbm, lag_hbm, lhs_out, lag_out,
    wave, table, keep, good,
    spec, mag, turn, sent, mid_a, mid_b, got, gram_in, cross, back_a, back_b, done_a, done_b, rows_f, lhs_f,
    send_sem, recv_sem, local_sem, load_sem,
):
    chan = lax.axis_index("chan")
    seg = lax.axis_index("seg")
    core = chan % 2
    y = (seg // 32) * 4 + chan // 2
    column = seg % 32
    z, x = column // 4, column % 4
    row = y * 2 + core
    y8 = (chan // 2) * 2 + seg // 32
    owner = share(row, column) != 0

    thirds = [pl.ds(256 * n, 256) for n in range(3)]
    loads = [
        pltpu.make_async_copy(src, dst, load_sem.at[n])
        for n, (src, dst) in enumerate(
            ((wave_hbm, wave), (table_hbm.at[thirds[0]], table.at[thirds[0]]), (keep_hbm, keep), (good_hbm, good),
             (table_hbm.at[thirds[1]], table.at[thirds[1]]), (table_hbm.at[thirds[2]], table.at[thirds[2]]))
        )
    ]
    for load in loads:
        load.start()

    def next_column(k):
        k = 32 - k
        return ((z + ring_8(k % 8)) % 8) * 4 + (x + ring_4(k // 8)) % 4

    def next_row(k):
        k = 16 - k
        return ((y + ring_8(k % 8)) % 8) * 2 + (core + k // 8) % 2

    barrier = pltpu.get_barrier_semaphore()

    @pl.loop(1, 32)
    def _(k):
        pl.semaphore_signal(barrier, inc=1, device_id=(chan, seg - column + (column + k) % 32), device_id_type=MESH)

    @pl.loop(1, 16)
    def _(k):
        pl.semaphore_signal(barrier, inc=1, device_id=device_of((row + k) % 16, column), device_id_type=MESH)

    def remote(src, dst, n, m, to_row, to_column):
        return pltpu.make_async_remote_copy(
            src_ref=src, dst_ref=dst, send_sem=send_sem.at[n], recv_sem=recv_sem.at[m],
            device_id=device_of(to_row, to_column), device_id_type=MESH,
        )

    def local(src, dst, n):
        return pltpu.make_async_copy(src, dst, local_sem.at[n])

    def wait_bytes(ref, sem):
        pltpu.make_async_copy(ref, ref, sem).wait()

    def loaded(third):
        for n in ((0, 1, 2, 3), (4,), (5,))[third]:
            loads[n].wait()

    def to_columns(c):
        @pl.loop(1, 32)
        def _(k):
            to = next_column(k)
            remote(sent.at[pl.ds(to * 12 + 6 * c, 6)], mid_a.at[column, pl.ds(6 * c, 6)], 0, c, row, to).start()

    def to_rows(to_core):
        @pl.loop(0, 8)
        def _(k):
            to = ((y + ring_8(7 - k)) % 8) * 2 + to_core

            @pl.when(to != row)
            def _():
                remote(sent.at[pl.ds(to * 24, 24)], mid_b.at[y8], 1, 2, to, column).start()

    def first_sends():
        pl.semaphore_wait(barrier, 46)

        @pl.when(core == 0)
        def _():
            to_columns(0)

        @pl.when(core == 1)
        def _():
            to_rows(0)

    make_units(core, wave, table, keep, good, spec, mag, turn, sent, loaded, first_sends)

    @pl.when(core == 0)
    def _():
        to_columns(1)
        local(sent.at[pl.ds(column * 12, 12)], mid_a.at[column], 0).start()

    @pl.when(core == 1)
    def _():
        to_rows(1)
        local(sent.at[pl.ds(row * 24, 24)], mid_b.at[y8], 1).start()

    pltpu.make_async_copy(lag_hbm, lag_out, load_sem.at[6]).start()

    def to_owners_in_column(to_core):
        @pl.loop(0, 8)
        def _(k):
            to = ((y + ring_8(7 - k)) % 8) * 2 + to_core

            @pl.when(jnp.logical_and(share(to, column) != 0, to != row))
            def _():
                remote(mid_a.at[:, column_slot(to, column)], got.at[0, y8], 2, 4, to, column).start()

    def to_owners_in_row():
        @pl.loop(1, 32)
        def _(k):
            to = next_column(k)

            @pl.when(share(row, to) != 0)
            def _():
                remote(mid_b.at[:, row_slot(row, to)], got.at[1, :, column], 3, 5, row, to).start()

    @pl.when(core == 0)
    def _():
        wait_bytes(mid_a.at[0], local_sem.at[0])
        wait_bytes(mid_a.at[pl.ds(0, 31), pl.ds(0, 6)], recv_sem.at[0])
        wait_bytes(mid_b, recv_sem.at[2])
        to_owners_in_row()
        to_owners_in_column(0)
        wait_bytes(mid_a.at[pl.ds(0, 31), pl.ds(0, 6)], recv_sem.at[1])
        to_owners_in_column(1)

    @pl.when(core == 1)
    def _():
        wait_bytes(mid_b.at[0], local_sem.at[1])
        wait_bytes(mid_b.at[pl.ds(0, 7)], recv_sem.at[2])
        to_owners_in_row()

    @pl.when(owner)
    def _():
        @pl.when(core == 0)
        def _():
            local(mid_a.at[:, column_slot(row, column)], got.at[0, y8], 2).start()

        local(mid_b.at[:, row_slot(row, column)], got.at[1, :, column], 3).start()
        @pl.when(core == 0)
        def _():
            wait_bytes(got.at[0, 0], local_sem.at[2])
            wait_bytes(got.at[0, pl.ds(0, 7)], recv_sem.at[4])

        @pl.when(core == 1)
        def _():
            wait_bytes(got.at[0], recv_sem.at[4])

        gather_blocks(0, got, gram_in)
        wait_bytes(got.at[1, :, 0], local_sem.at[3])
        wait_bytes(got.at[1, :, pl.ds(0, 31)], recv_sem.at[5])
        gather_blocks(1, got, gram_in)

        slot_a = row_slot(row, column) % 6
        slot_b = column_slot(row, column) % 6

        @pl.loop(0, 4)
        def _(step):
            pair = (quarter_of(step) + z // 2) % 4
            to_hi, half = (step // 2 + 1 - y // 4) % 2, step % 2
            first = jnp.where(core == 0, pair, to_hi * 4 + half)
            second = jnp.where(core == 0, pair + 4, to_hi * 4 + half + 2)
            cross_of(core, (first, second), gram_in, cross)

            @pl.when(core == 0)
            def _():
                @pl.loop(0, 8)
                def _(k):
                    to = pair * 8 + (column + k + 1) % 8
                    slot = step * 6 + slot_a

                    @pl.when(to != column)
                    def _():
                        remote(cross.at[pl.ds(to * 16, 16)], back_a.at[slot], 4, 6 + step // 2, row, to).start()

                    @pl.when(to == column)
                    def _():
                        local(cross.at[pl.ds(to * 16, 16)], back_a.at[slot], 4).start()

            @pl.when(core == 1)
            def _():
                @pl.loop(0, 8)
                def _(k):
                    to = to_hi * 8 + (row + k + 1) % 8
                    src = cross.at[pl.ds(to * 32 + half * 16, 16)]
                    dst = back_b.at[slot_b, pl.ds(half * 16, 16)]

                    @pl.when(to != row)
                    def _():
                        remote(src, dst, 5, 8 + half, to, column).start()

                    @pl.when(to == row)
                    def _():
                        local(src, dst, 5).start()

    own_a = jnp.logical_and(owner, core == 0)
    own_b = jnp.logical_and(owner, core == 1)

    @pl.when(own_b)
    def _():
        wait_bytes(back_b.at[0], local_sem.at[5])

    @pl.when(core == 0)
    def _():
        for c in range(2):
            if c == 1:
                @pl.when(own_a)
                def _():
                    wait_bytes(back_a.at[0], local_sem.at[4])
                    wait_bytes(back_a.at[pl.ds(0, 11)], recv_sem.at[7])

                @pl.when(jnp.logical_not(own_a))
                def _():
                    wait_bytes(back_a.at[pl.ds(0, 12)], recv_sem.at[7])
            else:
                wait_bytes(back_a.at[pl.ds(0, 12)], recv_sem.at[6])

            @pl.loop(1, 16)
            def _(k):
                to = next_row(k)
                slots = pl.ds(12 * c, 12)
                remote(back_a.at[slots, to], done_a.at[y, slots], 6, 10, to, column).start()

    for c in range(2):
        @pl.when(own_b)
        def _():
            wait_bytes(back_b.at[pl.ds(0, 5), pl.ds(0, 16)], recv_sem.at[8 + c])

        @pl.when(jnp.logical_not(own_b))
        def _():
            wait_bytes(back_b.at[:, pl.ds(0, 16)], recv_sem.at[8 + c])

        @pl.loop(0, 16)
        def _(k):
            place = (turned_column(column) + k + 1) % 16
            to = (place // 8) * 16 + c * 8 + place % 8

            @pl.when(to != column)
            def _():
                remote(back_b.at[:, place + 16 * c], done_b.at[column], 7, 11, row, to).start()

    @pl.when(core == 0)
    def _():
        local(back_a.at[:, row], done_a.at[y], 6).start()

    local(back_b.at[:, turned_column(column)], done_b.at[column], 7).start()

    @pl.when(core == 0)
    def _():
        wait_bytes(done_a.at[0], local_sem.at[6])
        wait_bytes(done_a.at[pl.ds(0, 7)], recv_sem.at[10])

    @pl.when(core == 1)
    def _():
        wait_bytes(done_a, recv_sem.at[10])

    wait_bytes(done_b.at[0], local_sem.at[7])
    wait_bytes(done_b.at[pl.ds(0, 31)], recv_sem.at[11])
    make_lhs(z // 2, done_a, done_b, rows_f, lhs_f, lhs_out)

    pltpu.make_async_copy(lag_hbm, lag_out, load_sem.at[6]).wait()

    @pl.when(core == 0)
    def _():
        wait_bytes(mid_a.at[pl.ds(0, 31)], send_sem.at[0])

        @pl.when(owner)
        def _():
            wait_bytes(got.at[0, pl.ds(0, 8)], send_sem.at[2])
            wait_bytes(got.at[0, pl.ds(0, 3)], send_sem.at[2])
            wait_bytes(cross.at[pl.ds(0, 31 * 16)], send_sem.at[4])

        @pl.when(jnp.logical_not(owner))
        def _():
            wait_bytes(got.at[0, pl.ds(0, 8)], send_sem.at[2])
            wait_bytes(got.at[0, pl.ds(0, 4)], send_sem.at[2])

        wait_bytes(done_a.at[pl.ds(0, 8)], send_sem.at[6])
        wait_bytes(done_a.at[pl.ds(0, 7)], send_sem.at[6])

    @pl.when(core == 1)
    def _():
        wait_bytes(sent.at[pl.ds(0, 15 * 24)], send_sem.at[1])

        @pl.when(owner)
        def _():
            wait_bytes(cross.at[pl.ds(0, 15 * 32)], send_sem.at[5])

    @pl.when(owner)
    def _():
        wait_bytes(got.at[1, :, pl.ds(0, 23)], send_sem.at[3])

    @pl.when(jnp.logical_not(owner))
    def _():
        wait_bytes(got.at[1, :, pl.ds(0, 24)], send_sem.at[3])

    wait_bytes(done_b.at[pl.ds(0, 31)], send_sem.at[7])


def stacked(wave, table, keep, good, lag):
    in_hbm = pl.BlockSpec(memory_space=pltpu.HBM)
    return pl.pallas_call(
        stack_kernel,
        out_shape=(pltpu.VMEM((512, 2 * BINS), BF16), pltpu.VMEM((2 * BINS, LAGS), BF16)),
        in_specs=[in_hbm] * 5,
        out_specs=(pl.BlockSpec(memory_space=pltpu.VMEM),) * 2,
        scratch_shapes=[
            pltpu.VMEM((512, NT), BF16),
            pltpu.VMEM((2 * BINS, NT), BF16),
            pltpu.SMEM((8,), jnp.int32),
            pltpu.VMEM((1, 64), jnp.int32),
            pltpu.VMEM((2 * BINS, 512), F32),
            pltpu.VMEM((BINS, 512), F32),
            pltpu.VMEM((BINS * 8, 128), F32),
            pltpu.VMEM((BINS, 8, 128), BF16),
            pltpu.VMEM((32, 12, 8, 128), BF16),
            pltpu.VMEM((8, 24, 8, 128), BF16),
            pltpu.VMEM((2, 8, 32, 8, 128), BF16),
            pltpu.VMEM((512, 1024), BF16),
            pltpu.VMEM((512, 8, 128), BF16),
            pltpu.VMEM((24, 16, 8, 128), BF16),
            pltpu.VMEM((6, 32, 8, 128), BF16),
            pltpu.VMEM((8, 24, 8, 128), BF16),
            pltpu.VMEM((32, 6, 8, 128), BF16),
            pltpu.VMEM((3072, 128), F32),
            pltpu.VMEM((6, 512, 128), F32),
            pltpu.SemaphoreType.DMA((8,)),
            pltpu.SemaphoreType.DMA((12,)),
            pltpu.SemaphoreType.DMA((8,)),
            pltpu.SemaphoreType.DMA((7,)),
        ],
        compiler_params=pltpu.CompilerParams(collective_id=0, has_side_effects=True, vmem_limit_bytes=48 << 20),
        name="stack_cross_spectra",
    )(*[pltpu.with_memory_space_constraint(value, pltpu.HBM) for value in (wave, table, keep, good, lag)])


def lag_kernel(scale, lhs, table, out, block, sem):
    width = 512
    copies = []
    for n in range(LAGS // width):
        cols = slice(n * width, (n + 1) * width)
        values = jnp.dot(lhs[...], table[:, cols], preferred_element_type=F32) * scale
        block[:, :, cols] = values.reshape(64, 8, width).astype(BF16)
        at = pl.ds(n * width, width)
        copies.append(pltpu.make_async_copy(block.at[:, :, at], out.at[:, :, at], sem.at[n]))
        copies[-1].start()
    for copy in copies:
        copy.wait()


def lagged(lhs, table, scale):
    vmem = pl.BlockSpec(memory_space=pltpu.VMEM)
    return pl.pallas_call(
        functools.partial(lag_kernel, scale),
        out_shape=jax.ShapeDtypeStruct((64, 8, LAGS), BF16),
        in_specs=[vmem, vmem],
        out_specs=pl.BlockSpec(memory_space=pl.ANY),
        scratch_shapes=[pltpu.VMEM((64, 8, LAGS), BF16), pltpu.SemaphoreType.DMA((5,))],
        compiler_params=pltpu.CompilerParams(vmem_limit_bytes=32 << 20),
        name="lag_transform",
    )(lhs, table)


def local(waveforms, segment_keep, channel_good):
    wave = waveforms.reshape(512, NT)
    lhs, lag = stacked(
        wave, jnp.asarray(forward_rows()), segment_keep, channel_good.reshape(1, 64), jnp.asarray(lag_rows())
    )
    return lagged(lhs, lag, float(1.0 / np.sqrt(SEGS * BINS)))


def solution(mesh):
    placed = (P("seg", "chan", None), P("seg"), P("chan"))
    return jax.shard_map(
        local, mesh=mesh, in_specs=placed, out_specs=P("chan", "seg", None), check_vma=False
    )
```

```python
import functools

import jax
import jax.numpy as jnp
import ml_dtypes
import numpy as np
from jax import lax
from jax.experimental import pallas as pl
from jax.experimental.pallas import tpu as pltpu
from jax.sharding import PartitionSpec as P

NT = 1536
BINS = 384
LOWEST = 12
LAGS = 2560
SEGS = 512
MESH = pl.DeviceIdType.MESH
F32 = jnp.float32
BF16 = jnp.bfloat16


def forward_rows():
    t = np.arange(NT, dtype=np.int64)
    f = LOWEST + np.arange(BINS, dtype=np.int64)
    theta = np.float32(2.0 * np.pi / (2 * NT)) * ((f[:, None] * t[None, :]) % (2 * NT)).astype(np.float32)
    theta = theta.astype(np.float64)
    rows = np.concatenate([np.cos(theta), -np.sin(theta)], axis=0) / np.sqrt(NT)
    return rows.astype(np.float32).astype(ml_dtypes.bfloat16)


def lag_rows():
    f = LOWEST + np.arange(BINS, dtype=np.int64)
    l = np.arange(LAGS, dtype=np.int64) - LAGS // 2
    phi = np.float32(2.0 * np.pi / (2 * NT)) * ((f[:, None] * l[None, :]) % (2 * NT)).astype(np.float32)
    phi = phi.astype(np.float64)
    rows = np.concatenate([np.cos(phi), -np.sin(phi)], axis=0)
    return rows.astype(np.float32).astype(ml_dtypes.bfloat16)


def device_of(row, column):
    y, core = row // 2, row % 2
    return ((y % 4) * 2 + core, (y // 4) * 32 + column)


def share(row, column):
    return (row // 2 + 2 * (row % 2) + column // 4 + column % 4) % 4


def column_slot(row, column):
    return (row % 2) * 6 + (row // 8) * 3 + share(row, column) - 1


def row_slot(row, column):
    return (column // 4) * 3 + share(row, column) - 1


def turned_column(column):
    return ((column // 8) % 2) * 16 + (column // 16) * 8 + column % 8


QUARTERS = (2, 1, 3, 0)


def quarter_of(step):
    return jnp.where(step == 0, 2, jnp.where(step == 1, 1, jnp.where(step == 2, 3, 0)))


def ring_8(k):
    return jnp.where(k % 2 == 1, (k + 1) // 2, (8 - k // 2) % 8)


def ring_4(k):
    return jnp.where(k == 2, 3, jnp.where(k == 3, 2, k))


def make_units(core, wave, table, keep, good, spec, mag, turn, sent, loaded=None, between=None):
    for third in range(3):
        if loaded is not None:
            loaded(third)
        rows = slice(256 * third, 256 * third + 256)
        spec[rows, :] = lax.dot_general(
            table[rows, :], wave[...], (((1,), (1,)), ((), ())), preferred_element_type=F32
        )

    def add_magnitude(g, total):
        at = pl.multiple_of(g * 8, 8)
        re = spec[pl.ds(at, 8), :]
        im = spec[pl.ds(pl.multiple_of(BINS + at, 8), 8), :]
        m = jnp.sqrt(re * re + im * im)
        mag[pl.ds(at, 8), :] = m
        return total + m

    total = lax.fori_loop(0, BINS // 8, add_magnitude, jnp.zeros((8, 512), F32), unroll=4)
    water = 0.5 * (jnp.sum(total, axis=0, keepdims=True) * (1.0 / BINS)) + 1e-06
    good_f = good[...].astype(F32)
    good_2 = jnp.concatenate([good_f, good_f], axis=1)
    lower = lax.broadcasted_iota(jnp.int32, (1, 128), 1) < 64
    flags = jnp.concatenate(
        [good_2 * jnp.where(lower, keep[2 * t].astype(F32), keep[2 * t + 1].astype(F32)) for t in range(4)], axis=1
    )
    lower8 = lax.broadcasted_iota(jnp.int32, (8, 128), 1) < 64

    def whiten_8(at):
        weight = flags / jnp.maximum(mag[pl.ds(at, 8), :], water)
        re = spec[pl.ds(at, 8), :] * weight
        im = spec[pl.ds(BINS + at, 8), :] * weight
        rows = at * 8
        for t in range(4):
            r_t, i_t = re[:, 128 * t : 128 * t + 128], im[:, 128 * t : 128 * t + 128]
            turn[pl.ds(rows + 2 * t, 8, stride=8), :] = jnp.where(lower8, r_t, pltpu.roll(i_t, 64, 1))
            turn[pl.ds(rows + 2 * t + 1, 8, stride=8), :] = jnp.where(lower8, pltpu.roll(r_t, 64, 1), i_t)

    def whiten_half(half):
        for block in range(24):
            whiten_8(half * 192 + 8 * block)

    def place_24(at, places):
        for k, place in enumerate(places):
            sent[place] = turn[pl.ds(pl.multiple_of(at * 8 + 8 * k, 8), 8), :].astype(BF16)

    whiten_half(0)

    @pl.when(core == 0)
    def _():
        @pl.loop(0, 8)
        def _(y0):
            x_base = [((c + 32 - y0) % 4) * 12 + (y0 // 4) * 3 for c in range(4)]
            places = []
            for slot in range(24):
                z0, r0 = slot // 3, slot % 3
                places.append(x_base[(r0 + 1 - z0) % 4] + (z0 * 48 + r0))
            place_24(pl.multiple_of(y0 * 24, 8), places)

    @pl.when(core == 1)
    def _():
        @pl.loop(0, 8)
        def _(y0):
            places = []
            for slot in range(24):
                places.append(y0 * 48 + slot)
            place_24(pl.multiple_of(y0 * 24, 8), places)

    if between is not None:
        between()

    whiten_half(1)

    @pl.when(core == 0)
    def _():
        @pl.loop(0, 8)
        def _(z1):
            places = []
            for n in range(24):
                x1, slot = n // 6, n % 6
                places.append(z1 * 48 + (x1 * 12 + 6 + slot))
            place_24(pl.multiple_of(192 + z1 * 24, 8), places)

    @pl.when(core == 1)
    def _():
        @pl.loop(0, 8)
        def _(z1):
            y_base = [((c + 32 - z1) % 4) * 48 + z1 * 3 for c in range(4)]
            places = []
            for n in range(24):
                x1, slot = n // 6, n % 6
                yh1, r1 = slot // 3, slot % 3
                places.append(y_base[(r1 + 1 - 2 - x1) % 4] + (yh1 * 192 + 24 + r1))
            place_24(pl.multiple_of(192 + z1 * 24, 8), places)


def gather_blocks(c, got, gram_in):
    for yl in range(4):
        block = got[c, 2 * yl : 2 * yl + 2].astype(F32).reshape(512, 128).astype(BF16)
        gram_in[:, 128 * (4 * c + yl) : 128 * (4 * c + yl) + 128] = block


def block_of(chan):
    return (chan % 2) * 4 + chan // 2


def cross_of(core, chans, gram_in, cross):
    sign = jnp.where(lax.broadcasted_iota(jnp.int32, (1, 128), 1) < 64, 1.0, -1.0).astype(F32)
    b_ids = lax.broadcasted_iota(jnp.int32, (64, 128), 0)
    a_ids = lax.broadcasted_iota(jnp.int32, (64, 128), 1) % 64
    same = b_ids == a_ids
    ids = [block_of(chan) for chan in chans]
    left = jnp.concatenate(
        [gram_in[:, pl.ds(pl.multiple_of(i * 128, 128), 128)] for i in ids], axis=1
    )
    products = lax.dot_general(left, gram_in[...], (((0,), (0,)), ((), ())), preferred_element_type=F32)
    for second in range(2):
        chan_b = chans[second]
        to_y, to_column = (chan_b // 4) * 4, (chan_b % 4) * 8
        base = jnp.where(core == 0, to_column * 16 + to_y * 2, to_y * 64 + turned_column(to_column))
        step_part = jnp.where(core == 0, 16, 1)
        step_row = jnp.where(core == 0, 1, 32)
        for j in range(8):
            tile = products[128 * second : 128 * second + 128, 128 * j : 128 * j + 128]
            summed = tile[:64] + sign * pltpu.roll(tile[64:], 64, 1)
            summed = jnp.where(jnp.logical_and(same, ids[second] == j), 0.0, summed)
            chan_a = (j % 4) * 2 + j // 4
            at = base + step_row * chan_a
            for part in range(8):
                cross[at + step_part * part] = summed[8 * part : 8 * part + 8].astype(BF16)


def make_lhs(z_pair, done_a, done_b, rows_f, lhs_f, lhs_out):
    for step in range(4):
        of_pair = (z_pair + 4 - QUARTERS[step]) % 4
        for y in range(8):
            values = done_a[y, 6 * step : 6 * step + 6].astype(F32).reshape(48, 128)
            rows_f[pl.ds(pl.multiple_of(of_pair * 48 + y * 192, 16), 48), :] = values
    rows_f[1536:3072] = done_b[...].astype(F32).reshape(1536, 128)
    for b in range(8):
        turned = rows_f[pl.ds(b, BINS, stride=8), :].T
        for p in range(2):
            for k in range(3):
                lhs_f[3 * p + k, pl.ds(b, 64, stride=8), :] = turned[64 * p : 64 * p + 64, 128 * k : 128 * k + 128]
    for k in range(6):
        lhs_out[:, 128 * k : 128 * k + 128] = lhs_f[k].astype(BF16)


def stack_kernel(
    wave_hbm, table_hbm, keep_hbm, good_hbm, lag_hbm, lhs_out, lag_out,
    wave, table, keep, good,
    spec, mag, turn, sent, mid_a, mid_b, got, gram_in, cross, back_a, back_b, done_a, done_b, rows_f, lhs_f,
    send_sem, recv_sem, local_sem, load_sem,
):
    chan = lax.axis_index("chan")
    seg = lax.axis_index("seg")
    core = chan % 2
    y = (seg // 32) * 4 + chan // 2
    column = seg % 32
    z, x = column // 4, column % 4
    row = y * 2 + core
    y8 = (chan // 2) * 2 + seg // 32
    owner = share(row, column) != 0

    thirds = [pl.ds(256 * n, 256) for n in range(3)]
    loads = [
        pltpu.make_async_copy(src, dst, load_sem.at[n])
        for n, (src, dst) in enumerate(
            ((wave_hbm, wave), (table_hbm.at[thirds[0]], table.at[thirds[0]]), (keep_hbm, keep), (good_hbm, good),
             (table_hbm.at[thirds[1]], table.at[thirds[1]]), (table_hbm.at[thirds[2]], table.at[thirds[2]]))
        )
    ]
    for load in loads:
        load.start()

    def next_column(k):
        k = 32 - k
        return ((z + ring_8(k % 8)) % 8) * 4 + (x + ring_4(k // 8)) % 4

    def next_row(k):
        k = 16 - k
        return ((y + ring_8(k % 8)) % 8) * 2 + (core + k // 8) % 2

    barrier = pltpu.get_barrier_semaphore()

    for k in range(1, 32):
        pl.semaphore_signal(barrier, inc=1, device_id=(chan, seg - column + (column + k) % 32), device_id_type=MESH)
    for k in range(1, 16):
        pl.semaphore_signal(barrier, inc=1, device_id=device_of((row + k) % 16, column), device_id_type=MESH)

    def remote(src, dst, n, m, to_row, to_column):
        return pltpu.make_async_remote_copy(
            src_ref=src, dst_ref=dst, send_sem=send_sem.at[n], recv_sem=recv_sem.at[m],
            device_id=device_of(to_row, to_column), device_id_type=MESH,
        )

    def local(src, dst, n):
        return pltpu.make_async_copy(src, dst, local_sem.at[n])

    def wait_bytes(ref, sem):
        pltpu.make_async_copy(ref, ref, sem).wait()

    def loaded(third):
        for n in ((0, 1, 2, 3), (4,), (5,))[third]:
            loads[n].wait()

    def to_columns(c):
        @pl.loop(1, 32)
        def _(k):
            to = next_column(k)
            remote(sent.at[pl.ds(to * 12 + 6 * c, 6)], mid_a.at[column, pl.ds(6 * c, 6)], 0, c, row, to).start()

    def to_rows(to_core):
        @pl.loop(0, 8)
        def _(k):
            to = ((y + ring_8(7 - k)) % 8) * 2 + to_core

            @pl.when(to != row)
            def _():
                remote(sent.at[pl.ds(to * 24, 24)], mid_b.at[y8], 1, 2, to, column).start()

    def first_sends():
        pl.semaphore_wait(barrier, 46)

        @pl.when(core == 0)
        def _():
            to_columns(0)

        @pl.when(core == 1)
        def _():
            to_rows(0)

    make_units(core, wave, table, keep, good, spec, mag, turn, sent, loaded, first_sends)

    @pl.when(core == 0)
    def _():
        to_columns(1)
        local(sent.at[pl.ds(column * 12, 12)], mid_a.at[column], 0).start()

    @pl.when(core == 1)
    def _():
        to_rows(1)
        local(sent.at[pl.ds(row * 24, 24)], mid_b.at[y8], 1).start()

    pltpu.make_async_copy(lag_hbm, lag_out, load_sem.at[6]).start()

    def to_owners_in_column(to_core):
        @pl.loop(0, 8)
        def _(k):
            to = ((y + ring_8(7 - k)) % 8) * 2 + to_core

            @pl.when(jnp.logical_and(share(to, column) != 0, to != row))
            def _():
                remote(mid_a.at[:, column_slot(to, column)], got.at[0, y8], 2, 4, to, column).start()

    def to_owners_in_row():
        @pl.loop(1, 32)
        def _(k):
            to = next_column(k)

            @pl.when(share(row, to) != 0)
            def _():
                remote(mid_b.at[:, row_slot(row, to)], got.at[1, :, column], 3, 5, row, to).start()

    @pl.when(core == 0)
    def _():
        wait_bytes(mid_a.at[0], local_sem.at[0])
        wait_bytes(mid_a.at[pl.ds(0, 31), pl.ds(0, 6)], recv_sem.at[0])
        wait_bytes(mid_b, recv_sem.at[2])
        to_owners_in_row()
        to_owners_in_column(0)
        wait_bytes(mid_a.at[pl.ds(0, 31), pl.ds(0, 6)], recv_sem.at[1])
        to_owners_in_column(1)

    @pl.when(core == 1)
    def _():
        wait_bytes(mid_b.at[0], local_sem.at[1])
        wait_bytes(mid_b.at[pl.ds(0, 7)], recv_sem.at[2])
        to_owners_in_row()

    @pl.when(owner)
    def _():
        @pl.when(core == 0)
        def _():
            local(mid_a.at[:, column_slot(row, column)], got.at[0, y8], 2).start()

        local(mid_b.at[:, row_slot(row, column)], got.at[1, :, column], 3).start()
        @pl.when(core == 0)
        def _():
            wait_bytes(got.at[0, 0], local_sem.at[2])
            wait_bytes(got.at[0, pl.ds(0, 7)], recv_sem.at[4])

        @pl.when(core == 1)
        def _():
            wait_bytes(got.at[0], recv_sem.at[4])

        gather_blocks(0, got, gram_in)
        wait_bytes(got.at[1, :, 0], local_sem.at[3])
        wait_bytes(got.at[1, :, pl.ds(0, 31)], recv_sem.at[5])
        gather_blocks(1, got, gram_in)

        slot_a = row_slot(row, column) % 6
        slot_b = column_slot(row, column) % 6

        @pl.loop(0, 4)
        def _(step):
            pair = (quarter_of(step) + z // 2) % 4
            to_hi, half = (step // 2 + 1 - y // 4) % 2, step % 2
            first = jnp.where(core == 0, pair, to_hi * 4 + half)
            second = jnp.where(core == 0, pair + 4, to_hi * 4 + half + 2)
            cross_of(core, (first, second), gram_in, cross)

            @pl.when(core == 0)
            def _():
                @pl.loop(0, 8)
                def _(k):
                    to = pair * 8 + (column + k + 1) % 8
                    slot = step * 6 + slot_a

                    @pl.when(to != column)
                    def _():
                        remote(cross.at[pl.ds(to * 16, 16)], back_a.at[slot], 4, 6 + step // 2, row, to).start()

                    @pl.when(to == column)
                    def _():
                        local(cross.at[pl.ds(to * 16, 16)], back_a.at[slot], 4).start()

            @pl.when(core == 1)
            def _():
                @pl.loop(0, 8)
                def _(k):
                    to = to_hi * 8 + (row + k + 1) % 8
                    src = cross.at[pl.ds(to * 32 + half * 16, 16)]
                    dst = back_b.at[slot_b, pl.ds(half * 16, 16)]

                    @pl.when(to != row)
                    def _():
                        remote(src, dst, 5, 8 + half, to, column).start()

                    @pl.when(to == row)
                    def _():
                        local(src, dst, 5).start()

    own_a = jnp.logical_and(owner, core == 0)
    own_b = jnp.logical_and(owner, core == 1)

    @pl.when(own_b)
    def _():
        wait_bytes(back_b.at[0], local_sem.at[5])

    @pl.when(core == 0)
    def _():
        for c in range(2):
            if c == 1:
                @pl.when(own_a)
                def _():
                    wait_bytes(back_a.at[0], local_sem.at[4])
                    wait_bytes(back_a.at[pl.ds(0, 11)], recv_sem.at[7])

                @pl.when(jnp.logical_not(own_a))
                def _():
                    wait_bytes(back_a.at[pl.ds(0, 12)], recv_sem.at[7])
            else:
                wait_bytes(back_a.at[pl.ds(0, 12)], recv_sem.at[6])

            @pl.loop(1, 16)
            def _(k):
                to = next_row(k)
                slots = pl.ds(12 * c, 12)
                remote(back_a.at[slots, to], done_a.at[y, slots], 6, 10, to, column).start()

    for c in range(2):
        @pl.when(own_b)
        def _():
            wait_bytes(back_b.at[pl.ds(0, 5), pl.ds(0, 16)], recv_sem.at[8 + c])

        @pl.when(jnp.logical_not(own_b))
        def _():
            wait_bytes(back_b.at[:, pl.ds(0, 16)], recv_sem.at[8 + c])

        @pl.loop(0, 16)
        def _(k):
            place = (turned_column(column) + k + 1) % 16
            to = (place // 8) * 16 + c * 8 + place % 8

            @pl.when(to != column)
            def _():
                remote(back_b.at[:, place + 16 * c], done_b.at[column], 7, 11, row, to).start()

    @pl.when(core == 0)
    def _():
        local(back_a.at[:, row], done_a.at[y], 6).start()

    local(back_b.at[:, turned_column(column)], done_b.at[column], 7).start()

    @pl.when(core == 0)
    def _():
        wait_bytes(done_a.at[0], local_sem.at[6])
        wait_bytes(done_a.at[pl.ds(0, 7)], recv_sem.at[10])

    @pl.when(core == 1)
    def _():
        wait_bytes(done_a, recv_sem.at[10])

    wait_bytes(done_b.at[0], local_sem.at[7])
    wait_bytes(done_b.at[pl.ds(0, 31)], recv_sem.at[11])
    make_lhs(z // 2, done_a, done_b, rows_f, lhs_f, lhs_out)

    pltpu.make_async_copy(lag_hbm, lag_out, load_sem.at[6]).wait()

    @pl.when(core == 0)
    def _():
        wait_bytes(mid_a.at[pl.ds(0, 31)], send_sem.at[0])

        @pl.when(owner)
        def _():
            wait_bytes(got.at[0, pl.ds(0, 8)], send_sem.at[2])
            wait_bytes(got.at[0, pl.ds(0, 3)], send_sem.at[2])
            wait_bytes(cross.at[pl.ds(0, 31 * 16)], send_sem.at[4])

        @pl.when(jnp.logical_not(owner))
        def _():
            wait_bytes(got.at[0, pl.ds(0, 8)], send_sem.at[2])
            wait_bytes(got.at[0, pl.ds(0, 4)], send_sem.at[2])

        wait_bytes(done_a.at[pl.ds(0, 8)], send_sem.at[6])
        wait_bytes(done_a.at[pl.ds(0, 7)], send_sem.at[6])

    @pl.when(core == 1)
    def _():
        wait_bytes(sent.at[pl.ds(0, 15 * 24)], send_sem.at[1])

        @pl.when(owner)
        def _():
            wait_bytes(cross.at[pl.ds(0, 15 * 32)], send_sem.at[5])

    @pl.when(owner)
    def _():
        wait_bytes(got.at[1, :, pl.ds(0, 23)], send_sem.at[3])

    @pl.when(jnp.logical_not(owner))
    def _():
        wait_bytes(got.at[1, :, pl.ds(0, 24)], send_sem.at[3])

    wait_bytes(done_b.at[pl.ds(0, 31)], send_sem.at[7])


def stacked(wave, table, keep, good, lag):
    in_hbm = pl.BlockSpec(memory_space=pltpu.HBM)
    return pl.pallas_call(
        stack_kernel,
        out_shape=(pltpu.VMEM((512, 2 * BINS), BF16), pltpu.VMEM((2 * BINS, LAGS), BF16)),
        in_specs=[in_hbm] * 5,
        out_specs=(pl.BlockSpec(memory_space=pltpu.VMEM),) * 2,
        scratch_shapes=[
            pltpu.VMEM((512, NT), BF16),
            pltpu.VMEM((2 * BINS, NT), BF16),
            pltpu.SMEM((8,), jnp.int32),
            pltpu.VMEM((1, 64), jnp.int32),
            pltpu.VMEM((2 * BINS, 512), F32),
            pltpu.VMEM((BINS, 512), F32),
            pltpu.VMEM((BINS * 8, 128), F32),
            pltpu.VMEM((BINS, 8, 128), BF16),
            pltpu.VMEM((32, 12, 8, 128), BF16),
            pltpu.VMEM((8, 24, 8, 128), BF16),
            pltpu.VMEM((2, 8, 32, 8, 128), BF16),
            pltpu.VMEM((512, 1024), BF16),
            pltpu.VMEM((512, 8, 128), BF16),
            pltpu.VMEM((24, 16, 8, 128), BF16),
            pltpu.VMEM((6, 32, 8, 128), BF16),
            pltpu.VMEM((8, 24, 8, 128), BF16),
            pltpu.VMEM((32, 6, 8, 128), BF16),
            pltpu.VMEM((3072, 128), F32),
            pltpu.VMEM((6, 512, 128), F32),
            pltpu.SemaphoreType.DMA((8,)),
            pltpu.SemaphoreType.DMA((12,)),
            pltpu.SemaphoreType.DMA((8,)),
            pltpu.SemaphoreType.DMA((7,)),
        ],
        compiler_params=pltpu.CompilerParams(collective_id=0, has_side_effects=True, vmem_limit_bytes=48 << 20),
        name="stack_cross_spectra",
    )(*[pltpu.with_memory_space_constraint(value, pltpu.HBM) for value in (wave, table, keep, good, lag)])


def lag_kernel(scale, lhs, table, out, block, sem):
    width = 512
    copies = []
    for n in range(LAGS // width):
        cols = slice(n * width, (n + 1) * width)
        values = jnp.dot(lhs[...], table[:, cols], preferred_element_type=F32) * scale
        block[:, :, cols] = values.reshape(64, 8, width).astype(BF16)
        at = pl.ds(n * width, width)
        copies.append(pltpu.make_async_copy(block.at[:, :, at], out.at[:, :, at], sem.at[n]))
        copies[-1].start()
    for copy in copies:
        copy.wait()


def lagged(lhs, table, scale):
    vmem = pl.BlockSpec(memory_space=pltpu.VMEM)
    return pl.pallas_call(
        functools.partial(lag_kernel, scale),
        out_shape=jax.ShapeDtypeStruct((64, 8, LAGS), BF16),
        in_specs=[vmem, vmem],
        out_specs=pl.BlockSpec(memory_space=pl.ANY),
        scratch_shapes=[pltpu.VMEM((64, 8, LAGS), BF16), pltpu.SemaphoreType.DMA((5,))],
        compiler_params=pltpu.CompilerParams(vmem_limit_bytes=32 << 20),
        name="lag_transform",
    )(lhs, table)


def local(waveforms, segment_keep, channel_good):
    wave = waveforms.reshape(512, NT)
    lhs, lag = stacked(
        wave, jnp.asarray(forward_rows()), segment_keep, channel_good.reshape(1, 64), jnp.asarray(lag_rows())
    )
    return lagged(lhs, lag, float(1.0 / np.sqrt(SEGS * BINS)))


def solution(mesh):
    placed = (P("seg", "chan", None), P("seg"), P("chan"))
    return jax.shard_map(
        local, mesh=mesh, in_specs=placed, out_specs=P("chan", "seg", None), check_vma=False
    )
```
